128 devices in a mesh: dp: 16 (over y, z), tp: 8 (over x, core).
Axes of the slice: x: 4, y: 4, z: 4, core: 2. Of those that a mesh axis runs over, the one named last changes fastest.
Arguments:
- cache_pool: bfloat16 [3072, 576, 128], P(('dp', 'tp')), may hold values from -4 to 4
- send_plan: int32 [128, 16, 2], P(('dp', 'tp')), may hold values from -1 to 23, as said below
- tables: int32 [512, 8], P(('dp', 'tp')), may hold values from 0 to 55, as said below
- lengths: int32 [512], P(('dp', 'tp')), may hold values from 385 to 1024
- new_latent: bfloat16 [2, 512, 576], P(None, ('dp', 'tp')), may hold values from -6 to 6
- queries: bfloat16 [2, 512, 64, 576], P(None, ('dp', 'tp')), may hold values from -20 to 20
- value_up: bfloat16 [64, 512, 128], P('dp'), may hold values from -0.25 to 0.25
- out_proj: bfloat16 [8192, 7168], P('dp'), may hold values from -0.0625 to 0.0625
- residual: bfloat16 [2, 512, 7168], P(None, ('dp', 'tp')), may hold values from -3 to 3
- norm_gain: float32 [7168], replicated, may hold values from 0.1 to 1.9
- routes: int32 [2, 512, 8], P(None, ('dp', 'tp')), may hold values from 0 to 31, all different within a row; in each aligned block of 4 rows (0 to 3, 4 to 7, ..., all dimensions but the last counted through in order) at most 2 rows name the same one
- route_weight: float32 [2, 512, 8], P(None, ('dp', 'tp')), may hold values from 0.05 to 0.6
- gate_proj: bfloat16 [32, 7168, 1024], P('dp', None, 'tp'), may hold values from -0.0625 to 0.0625
- up_proj: bfloat16 [32, 7168, 1024], P('dp', None, 'tp'), may hold values from -0.0625 to 0.0625
- down_proj: bfloat16 [32, 1024, 7168], P('dp', 'tp'), may hold values from -0.1875 to 0.1875
Outputs:
- layer_out: bfloat16 [2, 512, 7168], P(None, ('dp', 'tp'))
The draws below stay inside these ranges and needn't reach their ends.
Inputs may be any that keep to these rules, and one draw needn't show every extreme that they name: `send_plan`: -1 marks an empty slot. A device never lists one of its blocks twice. The blocks that a device sends to index g2 of dp fill its first slots for g2; it sends nothing to its own index of dp; it sends as many blocks in all as it receives; some device fills all 2 slots for a peer. `tables`: the first ceil(lengths[s] / 128) entries of a sequence's row name entries of its device's store after migration; over the device's sequences they name each of its own blocks that it does not send, and each received block that is not empty, exactly once; later entries are 0.
All inputs are finite; a program needn't handle non-finite values.
Results may differ from the reference program's by a relative error of at most 0.024.
Values may be sent and summed in bfloat16 or wider, within the bound.
A program may use at most 192 MiB of HBM per device.

```python
import math
import jax
import jax.numpy as jnp
import numpy as np
from jax import lax

D = 7168
HEADS = 64
LAT = 512
LATW = 576
VDIM = 128
BLK = 128
HID = 1024
TOP = 8
EXPERTS = 32
SEQ_DEV = 4
SEQS = 512
STEPS = 2
CAPM = 2
BLK_AVG = 6
POOL = 24
MAXB = 8
CAPT = 2
N_DP = 16
N_TP = 8


def latent_base(key):
    return jax.random.truncated_normal(key, -4.0, 4.0, (STEPS, SEQS, LATW), jnp.float32)


def migration_plan(key):
    device_count = N_DP * N_TP
    store_size = POOL + N_DP * CAPM
    key_pairs, key_leave, key_shuffle, key_split, key_tail = jax.random.split(key, 5)
    coin = jax.random.randint(key_pairs, (N_TP, N_DP, N_DP), 0, 2)
    upper = jnp.triu(coin, 1)
    counts = upper + jnp.swapaxes(upper, 1, 2)
    group_ids = jnp.arange(N_DP)
    beside = ((group_ids[:, None] + 1) % N_DP == group_ids[None, :]) | ((group_ids[None, :] + 1) % N_DP == group_ids[:, None])
    counts = jnp.where(beside[None], CAPM, counts)
    counts = jnp.where((group_ids[:, None] == group_ids[None, :])[None], 0, counts)
    per_device = jnp.transpose(counts, (1, 0, 2)).reshape(device_count, N_DP)
    leave_keys = jax.random.split(key_leave, device_count)
    leave_order = jax.vmap(lambda one_key: jax.random.permutation(one_key, POOL))(leave_keys)
    offsets = jnp.cumsum(per_device, axis=1) - per_device
    slot_ids = jnp.arange(CAPM)
    position = jnp.minimum(offsets[:, :, None] + slot_ids[None, None, :], POOL - 1)
    picked = jnp.take_along_axis(leave_order, position.reshape(device_count, N_DP * CAPM), axis=1).reshape(device_count, N_DP, CAPM)
    send = jnp.where(slot_ids[None, None, :] < per_device[:, :, None], picked, -1)
    departed = jnp.sum(per_device, axis=1)
    rank_of = jnp.argsort(leave_order, axis=1)
    keep_local = rank_of >= departed[:, None]
    incoming = jnp.transpose(counts, (2, 0, 1)).reshape(device_count, N_DP)
    arrived = (slot_ids[None, None, :] < incoming[:, :, None]).reshape(device_count, N_DP * CAPM)
    usable = jnp.concatenate([keep_local, arrived], axis=1)
    shuffle_keys = jax.random.split(key_shuffle, device_count)
    shuffle = jax.vmap(lambda one_key: jax.random.permutation(one_key, store_size))(shuffle_keys)
    ranking = jnp.where(usable, shuffle, store_size + jnp.arange(store_size)[None, :])
    store_order = jnp.argsort(ranking, axis=1)
    swing_most = BLK_AVG // 3
    swing = jax.random.randint(key_split, (device_count, SEQ_DEV // 2), 0, swing_most + 1)
    swing = swing.at[0, 0].set(swing_most)
    blocks = jnp.stack([BLK_AVG + swing, BLK_AVG - swing], axis=2).reshape(device_count, SEQ_DEV)
    starts = jnp.cumsum(blocks, axis=1) - blocks
    column = jnp.arange(MAXB)
    source_pos = jnp.minimum(starts[:, :, None] + column[None, None, :], store_size - 1)
    table = jnp.take_along_axis(store_order, source_pos.reshape(device_count, SEQ_DEV * MAXB), axis=1).reshape(device_count, SEQ_DEV, MAXB)
    table = jnp.where(column[None, None, :] < blocks[:, :, None], table, 0)
    tail = jax.random.randint(key_tail, (device_count, SEQ_DEV), 0, BLK)
    tail = tail.at[0, 0].set(0)
    seq_lengths = blocks * BLK - tail
    return (send, table.reshape(device_count * SEQ_DEV, MAXB), seq_lengths.reshape(device_count * SEQ_DEV))


def draw_send_plan(key, part):
    return migration_plan(key)[0].astype(jnp.int32)


def draw_tables(key, part):
    return migration_plan(key)[1].astype(jnp.int32)


def draw_lengths(key, part):
    return migration_plan(key)[2].astype(jnp.int32)


def draw_new_latent(key, part):
    base = latent_base(key)
    return base.astype(jnp.bfloat16)


def draw_queries(key, part):
    key = jax.random.fold_in(key, 12)
    key_main = jax.random.fold_in(key, 0)
    values = jax.random.truncated_normal(key_main, -4.0, 4.0, (STEPS, SEQS, HEADS, LATW), jnp.float32)
    return values.astype(jnp.bfloat16)


def block_scale(rng, shape, shards, low, high):
    def one(axis_at, parts):
        draws = jax.random.uniform(jax.random.fold_in(jax.random.fold_in(rng, 6), axis_at), (parts,), jnp.float32, low / len(shards), high / len(shards))
        return jnp.repeat(jnp.exp(draws), shape[axis_at] // parts).reshape((-1,) + (1,) * (len(shape) - axis_at - 1))

    gain = one(*shards[0])
    for cut in shards[1:]:
        gain = gain * one(*cut)
    return gain


def assign_block(rng, own, number, rows, amount, top, reach, lean):
    order = jax.random.permutation(rng, amount)
    crowded, common = portions_of(amount, rows * top, reach, lean, True), portions_of(amount, rows * top, reach, lean, False)
    places = jnp.arange(amount)

    def named(sizes, offset_by):
        used = int((sizes > 0).sum())
        fixed = max(1, used // 4)
        moved = fixed + (places - fixed + offset_by * (used - fixed)) % max(1, amount - fixed)
        return jnp.zeros((amount,), jnp.int32).at[order[jnp.where(places < fixed, places, moved)]].set(jnp.asarray(sizes, jnp.int32))

    sizes = jnp.where(number % 4 == 0, named(crowded, number // 4), named(common, number - number // 4 - 1))
    mixed = jax.random.permutation(jax.random.fold_in(own, 3), amount)
    source_of, sink = mixed[0:amount // 2 * 2:2], mixed[1:amount // 2 * 2:2]
    slack = jnp.minimum(sizes[source_of] - 1, reach - sizes[sink]) // 2
    slack = jnp.where((source_of == order[0]) | (sink == order[0]) | (sizes[sink] == 0), 0, jnp.maximum(slack, 0))
    moved = jax.random.randint(jax.random.fold_in(own, 4), (amount // 2,), 0, 1 << 20) % (slack + 1)
    sizes = sizes.at[source_of].add(-moved).at[sink].add(moved)
    items = jnp.searchsorted(jnp.cumsum(sizes), jnp.arange(rows * top), side="right").astype(jnp.int32)
    grid = items.reshape(top, rows).T
    grid = grid[jax.random.permutation(jax.random.fold_in(own, 1), rows)]
    offset_by = jax.random.randint(jax.random.fold_in(own, 2), (rows, 1), 0, top)
    return jnp.take_along_axis(grid, (jnp.arange(top)[None, :] + offset_by) % top, axis=1)


def portions_of(amount, total, reach, slope, full):
    loads = [(1 << 20) // math.isqrt(standing ** slope) + 1 for standing in range(1, amount + 1)]
    largest = reach if full else min(reach, max(-(-total // amount), total * loads[0] // sum(loads)))
    least = 1 if total - largest >= amount - 1 else 0
    given, spare = [largest] + [least] * (amount - 1), total - largest - least * (amount - 1)
    while spare > 0:
        movable = [i for i in range(1, amount) if given[i] < largest] or [i for i in range(1, amount) if given[i] < reach]
        mass, remaining = sum([loads[i] for i in movable]), spare
        for i in movable:
            extra = min(reach - given[i], max(1, remaining * loads[i] // mass), spare)
            given[i] = given[i] + extra
            spare = spare - extra
    return np.array(given)


def centred(rng, dims, deviation, reach, cuts=(), kind=jnp.bfloat16):
    drawn = deviation * jax.random.normal(rng, dims, jnp.float32)
    if cuts:
        drawn = drawn * block_scale(rng, dims, cuts, -0.22, 0.18)
    return jnp.clip(drawn, -reach, reach).astype(kind)


def setup_inputs(seed: int = 0) -> dict:
    key_of = jax.random.split(jax.random.key(seed), 16)
    cache_pool = centred(key_of[0], (N_DP * N_TP * POOL, LATW, BLK), 1.0, 4.0, ((0, 128),))
    send_plan = draw_send_plan(jax.random.fold_in(key_of[15], 71), 0)
    tables = draw_tables(jax.random.fold_in(key_of[15], 71), 0)
    lengths = draw_lengths(jax.random.fold_in(key_of[15], 71), 0)
    new_latent = draw_new_latent(jax.random.fold_in(key_of[15], 71), 0)
    queries = draw_queries(jax.random.fold_in(key_of[15], 71), 0)
    value_up = centred(key_of[6], (HEADS, LAT, VDIM), LAT ** -0.5, 0.25, ((0, 16),))
    out_proj = centred(key_of[7], (HEADS * VDIM, D), (HEADS * VDIM) ** -0.5, 0.0625, ((0, 16),))
    residual = centred(key_of[8], (STEPS, SEQS, D), 0.5, 3.0, ((1, 128),))
    norm_gain = jnp.clip(1.0 + 0.18 * jax.random.normal(key_of[9], (D,), jnp.float32), 0.1, 1.9)
    routes_keys = jax.random.split(jax.random.fold_in(key_of[10], 1), STEPS * SEQS // SEQ_DEV)
    routes_turns = jax.random.permutation(jax.random.fold_in(key_of[10], 3), STEPS * SEQS // SEQ_DEV)
    routes = jax.vmap(lambda own, number: assign_block(jax.random.fold_in(key_of[10], 2), own, number, SEQ_DEV, EXPERTS, TOP, CAPT, 2))(routes_keys, routes_turns).reshape((STEPS, SEQS, TOP))
    route_weight = jnp.clip(jnp.exp(math.log(0.6) - 2.4849067 * jax.random.uniform(key_of[11], (STEPS, SEQS, TOP), jnp.float32) ** block_scale(key_of[11], (STEPS, SEQS, TOP), ((1, 128),), -0.2, 0.2)), 0.05, 0.6)
    gate_proj = centred(key_of[12], (EXPERTS, D, HID), D ** -0.5, 0.0625, ((0, 16), (2, 8)))
    up_proj = centred(key_of[13], (EXPERTS, D, HID), D ** -0.5, 0.0625, ((0, 16), (2, 8)))
    down_proj = centred(key_of[14], (EXPERTS, HID, D), HID ** -0.5, 0.1875, ((0, 16), (1, 8)))
    return dict(cache_pool=cache_pool, send_plan=send_plan, tables=tables, lengths=lengths, new_latent=new_latent, queries=queries, value_up=value_up, out_proj=out_proj, residual=residual, norm_gain=norm_gain, routes=routes, route_weight=route_weight, gate_proj=gate_proj, up_proj=up_proj, down_proj=down_proj)


score_scale = 1.0 / 13.856406460551018
norm_eps = 1e-06

def attend(query_rows, cached_keys, usable_mask, fresh_keys):
    query_wide = query_rows.astype(jnp.float32)
    cached_wide = cached_keys.astype(jnp.float32)
    fresh_wide = fresh_keys.astype(jnp.float32)
    cache_scores = jnp.einsum('shc,sbci->shbi', query_wide, cached_wide) * score_scale
    cache_scores = jnp.where(usable_mask[:, None], cache_scores, -jnp.inf)
    fresh_scores = jnp.einsum('shc,ksc->shk', query_wide, fresh_wide) * score_scale
    largest = jnp.maximum(lax.optimization_barrier(jnp.max(cache_scores, axis=(2, 3))), lax.optimization_barrier(jnp.max(fresh_scores, axis=2)))
    cache_weights = jnp.exp(cache_scores - largest[:, :, None, None])
    fresh_weights = jnp.exp(fresh_scores - largest[:, :, None])
    denominator = lax.optimization_barrier(jnp.sum(cache_weights, axis=(2, 3))) + lax.optimization_barrier(jnp.sum(fresh_weights, axis=2))
    cache_probs = (cache_weights / denominator[:, :, None, None]).astype(jnp.bfloat16)
    fresh_probs = (fresh_weights / denominator[:, :, None]).astype(jnp.bfloat16)
    latent_sum = jnp.einsum('shbi,sbci->shc', cache_probs.astype(jnp.float32), cached_wide[:, :, :LAT, :])
    latent_sum = latent_sum + jnp.einsum('shk,ksc->shc', fresh_probs.astype(jnp.float32), fresh_wide[:, :, :LAT])
    return latent_sum.astype(jnp.bfloat16)

def moe_step(normed, expert_ids, weights, gate_proj, up_proj, down_proj):
    tile_rows = 32
    pair_count = SEQS * TOP
    flat_ids = expert_ids.reshape(-1).astype(jnp.int32)
    sort_order = jnp.argsort(flat_ids, stable=True).astype(jnp.int32)
    sorted_ids = flat_ids[sort_order]
    counts = lax.optimization_barrier(jnp.sum((flat_ids[None, :] == jnp.arange(EXPERTS, dtype=jnp.int32)[:, None]).astype(jnp.int32), axis=1))
    padded = (counts + tile_rows - 1) // tile_rows * tile_rows
    starts = jnp.cumsum(counts) - counts
    padded_ends = jnp.cumsum(padded)
    padded_starts = padded_ends - padded
    destination = (padded_starts[sorted_ids] + jnp.arange(pair_count, dtype=jnp.int32) - starts[sorted_ids]).astype(jnp.int32)
    tile_count = pair_count // tile_rows + EXPERTS
    row_token = jnp.full((tile_count * tile_rows,), -1, jnp.int32).at[destination].set(sort_order // TOP)
    tile_start = jnp.arange(tile_count, dtype=jnp.int32) * tile_rows
    tile_expert = jnp.minimum(lax.optimization_barrier(jnp.sum((padded_ends[None, :] <= tile_start[:, None]).astype(jnp.int32), axis=1)), EXPERTS - 1)
    share_width = HID // N_TP

    def run_tile(number):
        expert_id = tile_expert[number]
        token_ids = lax.dynamic_slice_in_dim(row_token, number * tile_rows, tile_rows)
        gathered_rows = jnp.where((token_ids >= 0)[:, None], normed[jnp.maximum(token_ids, 0)], jnp.zeros((), jnp.bfloat16))
        gate_act = jnp.dot(gathered_rows, gate_proj[expert_id], preferred_element_type=jnp.float32)
        up_act = jnp.dot(gathered_rows, up_proj[expert_id], preferred_element_type=jnp.float32)
        hidden = (jax.nn.silu(gate_act) * up_act).astype(jnp.bfloat16)
        hidden_parts = hidden.reshape(tile_rows, N_TP, share_width).astype(jnp.float32)
        down_parts = down_proj[expert_id].reshape(N_TP, share_width, D).astype(jnp.float32)
        partial_value = jnp.einsum('rpk,pkd->rpd', hidden_parts, down_parts)
        partial_value = lax.optimization_barrier(partial_value.astype(jnp.bfloat16)).astype(jnp.float32)
        return lax.optimization_barrier(jnp.sum(partial_value, axis=1))
    outputs = lax.map(run_tile, jnp.arange(tile_count, dtype=jnp.int32)).reshape(tile_count * tile_rows, D)
    pair_dest = jnp.zeros((pair_count,), jnp.int32).at[sort_order].set(destination)
    per_pair = outputs[pair_dest].reshape(SEQS, TOP, D)
    return lax.optimization_barrier(jnp.sum(per_pair * weights[:, :, None].astype(jnp.float32), axis=1))

def reference(cache_pool, send_plan, tables, lengths, new_latent, queries, value_up, out_proj, residual, norm_gain, routes, route_weight, gate_proj, up_proj, down_proj):
    device_count = N_DP * N_TP
    stores_all = cache_pool.reshape(device_count, POOL, LATW, BLK)
    token_position = (jnp.arange(MAXB, dtype=jnp.int32)[:, None] * BLK + jnp.arange(BLK, dtype=jnp.int32)[None, :]).astype(jnp.int32)

    def one_device(device):
        group_index = device // N_TP
        lane_index = device % N_TP
        source_ids = (jnp.arange(N_DP, dtype=jnp.int32) * N_TP + lane_index).astype(jnp.int32)
        listed_ids = send_plan[source_ids, group_index]
        moved_blocks = stores_all[source_ids[:, None], jnp.maximum(listed_ids, 0)]
        moved_blocks = jnp.where((listed_ids >= 0)[:, :, None, None], moved_blocks, jnp.zeros((), jnp.bfloat16))
        combined = jnp.concatenate([stores_all[device], moved_blocks.reshape(N_DP * CAPM, LATW, BLK)], axis=0)
        seq_rows = (device * SEQ_DEV + jnp.arange(SEQ_DEV, dtype=jnp.int32)).astype(jnp.int32)
        gathered = combined[tables[seq_rows]]
        usable_mask = token_position[None] < lengths[seq_rows][:, None, None]
        fresh_keys = new_latent[:, seq_rows]
        results = []
        for step_no in range(STEPS):
            results.append(attend(queries[step_no][seq_rows], gathered, usable_mask, fresh_keys[:step_no + 1]))
        return jnp.stack(results)
    latent = lax.map(one_device, jnp.arange(device_count, dtype=jnp.int32))
    latent = jnp.transpose(latent, (1, 0, 2, 3, 4)).reshape(STEPS, SEQS, HEADS, LAT)
    per_head = jnp.einsum('kshc,hcv->kshv', latent.astype(jnp.float32), value_up.astype(jnp.float32)).astype(jnp.bfloat16)
    head_flat = per_head.reshape(STEPS * SEQS, HEADS * VDIM)
    attention = jnp.dot(head_flat, out_proj, preferred_element_type=jnp.float32).reshape(STEPS, SEQS, D)
    stream = (residual.astype(jnp.float32) + attention).astype(jnp.bfloat16)
    stream_wide = stream.astype(jnp.float32)
    mean_square = lax.optimization_barrier(jnp.mean(stream_wide * stream_wide, axis=-1, keepdims=True))
    normed = (stream_wide * lax.rsqrt(mean_square + norm_eps) * norm_gain).astype(jnp.bfloat16)
    mixture = jnp.stack([moe_step(normed[step_no], routes[step_no], route_weight[step_no], gate_proj, up_proj, down_proj) for step_no in range(STEPS)])
    return (stream_wide + mixture).astype(jnp.bfloat16)
```

```python
import functools

import jax
import jax.numpy as jnp
from jax import lax
from jax.experimental import pallas as pl
from jax.experimental.pallas import tpu as pltpu
from jax.sharding import PartitionSpec as P

MESH = pl.DeviceIdType.MESH
F32 = jnp.float32
BF16 = jnp.bfloat16
LAT = 512
SCALE = 1.0 / 13.856406460551018
EPS = 1e-06
MIB = 1 << 20


def dot(a, b):
    return jnp.dot(a, b, preferred_element_type=F32)


def dot_nt(a, b):
    return lax.dot_general(a, b, (((1,), (1,)), ((), ())), preferred_element_type=F32)


def attention_kernel(
    plan, tab, lens, pool, queries, fresh, value_up, proj_hbm, resid, gain,
    stream_out, normed_out,
    outgoing, arrived, keys, lat_send, lat_recv, proj, part_send, part_recv,
    mig_send, mig_recv, lat_s, lat_r, part_s, part_r, local_sem,
):
    groups = 16
    me = lax.axis_index("dp")
    lane = lax.axis_index("tp")
    model = proj_hbm.shape[1]

    proj_copy = pltpu.make_async_copy(proj_hbm, proj, local_sem.at[0])
    proj_copy.start()

    barrier = pltpu.get_barrier_semaphore()
    for shift in range(1, groups):
        pl.semaphore_signal(
            barrier, inc=1, device_id=(lax.rem(me + shift, groups), lane), device_id_type=MESH
        )

    def pick(i, carry):
        outgoing[i] = pool[jnp.maximum(plan[i], 0)]
        return carry

    lax.fori_loop(0, 2 * groups, pick, 0)
    pl.semaphore_wait(barrier, groups - 1)

    def exchange(src, dst, send_sem, recv_sem, shift):
        peer = lax.rem(me + shift, groups)
        return pltpu.make_async_remote_copy(
            src_ref=src(peer),
            dst_ref=dst(me),
            send_sem=send_sem.at[shift - 1],
            recv_sem=recv_sem.at[shift - 1],
            device_id=(peer, lane),
            device_id_type=MESH,
        )

    moves = [
        exchange(
            lambda p: outgoing.at[pl.ds(2 * p, 2)],
            lambda m: arrived.at[pl.ds(2 * m, 2)],
            mig_send, mig_recv, shift,
        )
        for shift in range(1, groups)
    ]
    for move in moves:
        move.start()
    arrived[2 * me] = outgoing[2 * me]
    arrived[2 * me + 1] = outgoing[2 * me + 1]
    for move in moves:
        move.wait()

    row = lax.broadcasted_iota(jnp.int32, (128, 128), 0)
    col = lax.broadcasted_iota(jnp.int32, (128, 128), 1)
    reorder = jnp.where(
        col == ((row >> 2) & 1) * 64 + (row >> 3) * 4 + (row & 3), 1.0, 0.0
    ).astype(BF16)
    second_step = ((lax.broadcasted_iota(jnp.int32, (128, 1), 0) >> 2) & 1) == 1
    position = lax.broadcasted_iota(jnp.int32, (128, 1024), 1)

    def attend(s, carry):
        for j in range(8):
            entry = tab[s * 8 + j]
            own = pool[jnp.minimum(entry, 23)]
            moved = arrived[jnp.maximum(entry - 24, 0)]
            keys[:, j * 128:(j + 1) * 128] = jnp.where(entry < 24, own, moved)
        q = jnp.concatenate([queries[0, s], queries[1, s]], axis=0)
        q = dot(reorder, q)
        q16 = q.astype(BF16)
        scores = dot(q16, keys[...]) * SCALE
        scores = jnp.where(position < lens[s], scores, -jnp.inf)
        new = fresh[s]
        first = jnp.sum(q * new[0:1], axis=1, keepdims=True) * SCALE
        second = jnp.sum(q * new[1:2], axis=1, keepdims=True) * SCALE
        second = jnp.where(second_step, second, -jnp.inf)
        largest = jnp.maximum(jnp.max(scores, axis=1, keepdims=True), jnp.maximum(first, second))
        weights = jnp.exp(scores - largest)
        first = jnp.exp(first - largest)
        second = jnp.exp(second - largest)
        total = jnp.sum(weights, axis=1, keepdims=True) + first + second
        probs = (weights / total).astype(BF16)
        first = (first / total).astype(BF16).astype(F32)
        second = (second / total).astype(BF16).astype(F32)
        latent = dot_nt(probs, keys[0:LAT, :])
        latent = latent + first * new[0:1, 0:LAT] + second * new[1:2, 0:LAT]
        lat_send[:, pl.ds(s, 1)] = latent.reshape(16, 1, 8, LAT).astype(BF16)
        return carry

    lax.fori_loop(0, 4, attend, 0)

    moves = [
        exchange(lambda p: lat_send.at[p], lambda m: lat_recv.at[m], lat_s, lat_r, shift)
        for shift in range(1, groups)
    ]
    for move in moves:
        move.start()
    lat_recv[me] = lat_send[me]
    for move in moves:
        move.wait()

    rows = lat_recv[...].astype(F32).reshape(512, LAT).astype(BF16)
    row = lax.broadcasted_iota(jnp.int32, (128, 512), 0)
    col = lax.broadcasted_iota(jnp.int32, (128, 512), 1)
    base = (row >> 3) * 32 + (row & 3) * 8 + ((row >> 2) & 1) * 4
    heads = []
    for h in range(4):
        up = dot(rows, value_up[h]).astype(BF16)
        take = jnp.where(col == base + h, 1.0, 0.0).astype(BF16)
        heads.append(dot(take, up).astype(BF16))
    heads = jnp.concatenate(heads, axis=1)
    proj_copy.wait()
    chunk = 1024
    for n in range(model // chunk):
        cols = pl.ds(n * chunk, chunk)
        part_send[:, :, cols] = dot(heads, proj[:, cols]).reshape(16, 8, chunk).astype(BF16)

    moves = [
        exchange(lambda p: part_send.at[p], lambda m: part_recv.at[m], part_s, part_r, shift)
        for shift in range(1, groups)
    ]
    for move in moves:
        move.start()
    part_recv[me] = part_send[me]
    for move in moves:
        move.wait()

    square = jnp.zeros((8, 1), F32)
    for n in range(model // chunk):
        cols = pl.ds(n * chunk, chunk)
        total = resid[:, cols].astype(F32) + jnp.sum(part_recv[:, :, cols].astype(F32), axis=0)
        stream = total.astype(BF16)
        stream_out[:, cols] = stream
        wide = stream.astype(F32)
        square = square + jnp.sum(wide * wide, axis=1, keepdims=True)
    scale = lax.rsqrt(square * (1.0 / model) + EPS)
    for n in range(model // chunk):
        cols = pl.ds(n * chunk, chunk)
        wide = stream_out[:, cols].astype(F32)
        normed_out[:, cols] = (wide * scale * gain[:, cols]).astype(BF16)


PARTS = ((0, 2432), (2432, 2432), (4864, 2432))
OUT_PARTS = ((0, 2432), (2432, 2432), (4864, 2304))
ROW = 7296


def halves(start, width):
    tiles = width // 128
    first = (tiles + 1) // 2 * 128
    return (start, first), (start + first, width - first)


def expert_kernel(
    normed, mix, stream, gate, up, down,
    out,
    rows_buf, rows, hid_w, down_w, acc, obuf,
    h0l, h0r, f0l, f0r, h1l, h1r, f1l, f1r, h2l, h2r, f2l, f2r,
    ag_send, ag_recv, rs_send, rs_recv, w_send, w_recv, w_local,
):
    dp = lax.axis_index("dp")
    tp = lax.axis_index("tp")
    at = (dp // 4, dp % 4, tp // 2)
    core = tp % 2

    def neighbour(axis, sign):
        new = list(at)
        new[axis] = (at[axis] + sign + 4) % 4
        return (new[0] * 4 + new[1], new[2] * 2 + core)

    partner = (dp, (tp // 2) * 2 + (1 - core))

    barrier = pltpu.get_barrier_semaphore()
    for axis in range(3):
        for sign in (1, -1):
            pl.semaphore_signal(
                barrier, inc=1, device_id=neighbour(axis, sign), device_id_type=MESH
            )
    pl.semaphore_signal(barrier, inc=1, device_id=partner, device_id_type=MESH)

    rows_buf[at[0], at[1], at[2], :, 0:7168] = normed[...]
    rows_buf[at[0], at[1], at[2], :, 7168:7296] = mix[...]
    local = []
    remote = []

    def spots(e, which):
        if which < 2:
            base = e * 512 + which * 256
            return (
                hid_w.at[:, pl.ds(base, 128)],
                hid_w.at[:, pl.ds(base + 128, 128)],
            )
        return (
            down_w.at[pl.ds(e * 256, 128)],
            down_w.at[pl.ds(e * 256 + 128, 128)],
        )

    for e in range(2):
        for which, ref in enumerate((gate, up, down)):
            mine, theirs = spots(e, which)
            n = e * 3 + which
            local.append(pltpu.make_async_copy(ref.at[e], mine, w_local.at[n]))
            remote.append(
                pltpu.make_async_remote_copy(
                    src_ref=ref.at[e],
                    dst_ref=theirs,
                    send_sem=w_send.at[n],
                    recv_sem=w_recv.at[n],
                    device_id=partner,
                    device_id_type=MESH,
                )
            )
    for copy in local:
        copy.start()
    pl.semaphore_wait(barrier, 7)

    order = [(p, (p + 1) % 3, (p + 2) % 3) for p in range(3)]

    def place(known, axis, value):
        where = [at[0], at[1], at[2]]
        for a in known:
            where[a] = slice(None)
        where[axis] = value
        return tuple(where)

    def push(ref, dst, sends, recvs, slot, axis, sign):
        return pltpu.make_async_remote_copy(
            src_ref=ref,
            dst_ref=dst,
            send_sem=sends.at[slot],
            recv_sem=recvs.at[slot],
            device_id=neighbour(axis, sign),
            device_id_type=MESH,
        )

    for phase in range(3):
        ones = []
        for p in range(3):
            axis = order[p][phase]
            known = order[p][:phase]
            start, width = PARTS[p]
            own = place(known, axis, at[axis]) + (slice(None), pl.ds(start, width))
            slot = (phase * 3 + p) * 4
            pair = [
                push(rows_buf.at[own], rows_buf.at[own], ag_send, ag_recv, slot + k, axis, sign)
                for k, sign in enumerate((1, -1))
            ]
            for copy in pair:
                copy.start()
            ones.append(pair)
        if phase == 0:
            for copy in remote:
                copy.start()
        twos = []
        for p in range(3):
            axis = order[p][phase]
            known = order[p][:phase]
            slot = (phase * 3 + p) * 4 + 2
            pair = []
            for k, sign in enumerate((1, -1)):
                ones[p][k].wait_recv()
                start, width = halves(*PARTS[p])[k]
                came = place(known, axis, (at[axis] - sign + 4) % 4) + (
                    slice(None), pl.ds(start, width),
                )
                copy = push(
                    rows_buf.at[came], rows_buf.at[came], ag_send, ag_recv, slot + k, axis, sign
                )
                copy.start()
                pair.append(copy)
            twos.append(pair)
        for p in range(3):
            for k in range(2):
                ones[p][k].wait_send()
                twos[p][k].wait()

    for copy in local:
        copy.wait()
    for copy in remote:
        copy.wait()

    for y in range(4):
        rows[pl.ds(y * 128, 128), :] = (
            rows_buf[y].astype(F32).reshape(128, ROW).astype(BF16)
        )
    for n in range(4):
        cols = pl.ds(n * 256, 256)
        acc[:, cols] = dot(rows[:, 0:7168], hid_w[:, cols])
    lanes = lax.broadcasted_iota(jnp.int32, (512, 128), 1)
    table = rows[:, 7168:7296].astype(F32)
    hidden = []
    for e in range(2):
        expert = dp * 2 + e
        mine = (lanes == expert) | (lanes == expert + 32)
        weight = jnp.sum(jnp.where(mine, table, 0.0), axis=1, keepdims=True)
        gate_act = acc[:, e * 512:e * 512 + 256]
        up_act = acc[:, e * 512 + 256:e * 512 + 512]
        hidden.append((gate_act / (1.0 + jnp.exp(-gate_act)) * up_act * weight).astype(BF16))
    hidden = jnp.concatenate(hidden, axis=1)

    half_in = ((h0l, h0r), (h1l, h1r), (h2l, h2r))
    full_in = ((f0l, f0r), (f1l, f1r), (f2l, f2r))

    def half_dst(phase, p, k):
        ref = half_in[phase][k]
        _, width = halves(*OUT_PARTS[p])[k]
        return ref.at[(p,) + (slice(None),) * (3 - phase) + (pl.ds(0, width),)]

    def full_dst(phase, p, k):
        ref = full_in[phase][k]
        return ref.at[(p,) + (slice(None),) * (3 - phase) + (pl.ds(0, OUT_PARTS[p][1]),)]

    def first_sends(phase, p):
        axis = order[p][2 - phase]
        known = order[p][:2 - phase]
        pair = []
        for k, sign in enumerate((1, -1)):
            start, width = halves(*OUT_PARTS[p])[k]
            far = place(known, axis, (at[axis] + 2) % 4) + (slice(None), pl.ds(start, width))
            copy = push(
                obuf.at[far], half_dst(phase, p, k), rs_send, rs_recv,
                (phase * 3 + p) * 4 + k, axis, sign,
            )
            copy.start()
            pair.append(copy)
        return pair

    ones = []
    for phase in range(3):
        if phase == 0:
            for p in range(3):
                start, width = OUT_PARTS[p]
                done = 0
                while done < width:
                    size = min(256, width - done)
                    cols = pl.ds(start + done, size)
                    obuf[:, :, :, :, cols] = (
                        dot(hidden, down_w[:, cols]).reshape(4, 4, 4, 8, size).astype(BF16)
                    )
                    done += size
                ones.append(first_sends(0, p))
        else:
            ones = [first_sends(phase, p) for p in range(3)]
        twos = []
        for p in range(3):
            axis = order[p][2 - phase]
            known = order[p][:2 - phase]
            pair = []
            for k, sign in enumerate((1, -1)):
                ones[p][k].wait_recv()
                start, width = halves(*OUT_PARTS[p])[k]
                near = place(known, axis, (at[axis] + sign + 4) % 4)
                part = near + (slice(None), pl.ds(start, width))
                obuf[part] = (
                    obuf[part].astype(F32) + half_dst(phase, p, k)[...].astype(F32)
                ).astype(BF16)
                whole = near + (slice(None), pl.ds(*OUT_PARTS[p]))
                copy = push(
                    obuf.at[whole], full_dst(phase, p, k), rs_send, rs_recv,
                    (phase * 3 + p) * 4 + 2 + k, axis, sign,
                )
                copy.start()
                pair.append(copy)
            twos.append(pair)
        for p in range(3):
            axis = order[p][2 - phase]
            known = order[p][:2 - phase]
            for k in range(2):
                ones[p][k].wait_send()
                twos[p][k].wait()
            start, width = OUT_PARTS[p]
            own = place(known, axis, at[axis]) + (slice(None), pl.ds(start, width))
            total = (
                obuf[own].astype(F32)
                + full_dst(phase, p, 0)[...].astype(F32)
                + full_dst(phase, p, 1)[...].astype(F32)
            )
            if phase < 2:
                obuf[own] = total.astype(BF16)
            else:
                cols = pl.ds(start, width)
                out[:, cols] = (total + stream[:, cols].astype(F32)).astype(BF16)


def per_device(
    cache_pool, send_plan, tables, lengths, new_latent, queries, value_up, out_proj, residual,
    norm_gain, routes, route_weight, gate_proj, up_proj, down_proj,
):
    model = residual.shape[2]
    vmem = pl.BlockSpec(memory_space=pltpu.VMEM)
    smem = pl.BlockSpec(memory_space=pltpu.SMEM)
    hbm = pl.BlockSpec(memory_space=pl.ANY)
    dma = pltpu.SemaphoreType.DMA

    fresh = jnp.transpose(new_latent, (1, 0, 2)).astype(F32)
    resid = residual.reshape(8, model)
    stream, normed = pl.pallas_call(
        attention_kernel,
        out_shape=(
            jax.ShapeDtypeStruct((8, model), BF16),
            jax.ShapeDtypeStruct((8, model), BF16),
        ),
        in_specs=[smem, smem, smem, vmem, vmem, vmem, vmem, hbm, vmem, vmem],
        out_specs=(vmem, vmem),
        scratch_shapes=[
            pltpu.VMEM((32, 576, 128), BF16),
            pltpu.VMEM((32, 576, 128), BF16),
            pltpu.VMEM((576, 1024), BF16),
            pltpu.VMEM((16, 4, 8, LAT), BF16),
            pltpu.VMEM((16, 4, 8, LAT), BF16),
            pltpu.VMEM((512, model), BF16),
            pltpu.VMEM((16, 8, model), BF16),
            pltpu.VMEM((16, 8, model), BF16),
            dma((15,)), dma((15,)), dma((15,)), dma((15,)), dma((15,)), dma((15,)),
            dma((1,)),
        ],
        compiler_params=pltpu.CompilerParams(
            collective_id=0, has_side_effects=True, vmem_limit_bytes=56 * MIB
        ),
        name="attention",
    )(
        send_plan.reshape(-1), tables.reshape(-1), lengths, cache_pool, queries, fresh, value_up,
        out_proj, resid, norm_gain.reshape(1, model),
    )

    matches = routes.reshape(8, 8)[:, :, None] == jnp.arange(32, dtype=jnp.int32)[None, None, :]
    dense = jnp.sum(jnp.where(matches, route_weight.reshape(8, 8)[:, :, None], 0.0), axis=1)
    high = lax.reduce_precision(dense, 8, 7)
    mix = jnp.concatenate([high, dense - high, jnp.zeros((8, 64), F32)], axis=1).astype(BF16)

    def rings(shape, width):
        return [pltpu.VMEM((3,) + shape + (8, width), BF16)] * 2

    scratch = [
        pltpu.VMEM((4, 4, 4, 8, ROW), BF16),
        pltpu.VMEM((512, ROW), BF16),
        pltpu.VMEM((model, 1024), BF16),
        pltpu.VMEM((512, model), BF16),
        pltpu.VMEM((512, 1024), F32),
        pltpu.VMEM((4, 4, 4, 8, model), BF16),
    ]
    for shape in ((4, 4), (4,), ()):
        scratch += rings(shape, 1280)
        scratch += rings(shape, 2432)
    scratch += [dma((36,)), dma((36,)), dma((36,)), dma((36,)), dma((6,)), dma((6,)), dma((6,))]
    result = pl.pallas_call(
        expert_kernel,
        out_shape=jax.ShapeDtypeStruct((8, model), BF16),
        in_specs=[vmem, vmem, vmem, hbm, hbm, hbm],
        out_specs=vmem,
        scratch_shapes=scratch,
        compiler_params=pltpu.CompilerParams(
            collective_id=1, has_side_effects=True, vmem_limit_bytes=60 * MIB
        ),
        name="experts",
    )(normed, mix, stream, gate_proj, up_proj, down_proj)
    return result.reshape(residual.shape)


def solution(mesh):
    placed = (
        P(("dp", "tp"), None, None),
        P(("dp", "tp"), None, None),
        P(("dp", "tp"), None),
        P(("dp", "tp")),
        P(None, ("dp", "tp"), None),
        P(None, ("dp", "tp"), None, None),
        P("dp", None, None),
        P("dp", None),
        P(None, ("dp", "tp"), None),
        P(),
        P(None, ("dp", "tp"), None),
        P(None, ("dp", "tp"), None),
        P("dp", None, "tp"),
        P("dp", None, "tp"),
        P("dp", "tp", None),
    )
    return jax.shard_map(
        per_device,
        mesh=mesh,
        in_specs=placed,
        out_specs=P(None, ("dp", "tp"), None),
        check_vma=False,
    )
```

```python
import functools

import jax
import jax.numpy as jnp
from jax import lax
from jax.experimental import pallas as pl
from jax.experimental.pallas import tpu as pltpu
from jax.sharding import PartitionSpec as P

MESH = pl.DeviceIdType.MESH
F32 = jnp.float32
BF16 = jnp.bfloat16
LAT = 512
SCALE = 1.0 / 13.856406460551018
EPS = 1e-06
MIB = 1 << 20


def dot(a, b):
    return jnp.dot(a, b, preferred_element_type=F32)


def dot_nt(a, b):
    return lax.dot_general(a, b, (((1,), (1,)), ((), ())), preferred_element_type=F32)


def halves(start, width):
    tiles = width // 128
    first = (tiles + 1) // 2 * 128
    return (start, first), (start + first, width - first)


def ring_sum(at, orders, parts, buf, half_in, full_in, sends, recvs, neighbour, produce, finish):
    axes = len(orders[0])
    count = len(parts)

    def place(reduced, axis, value):
        where = [slice(None)] * axes
        for a in reduced:
            where[a] = at[a]
        where[axis] = value
        return tuple(where)

    def landing(refs, phase, p, k, width):
        return refs[phase][k].at[(p,) + (slice(None),) * (axes - phase) + (pl.ds(0, width),)]

    def push(src, dst, slot, axis, sign):
        copy = pltpu.make_async_remote_copy(
            src_ref=src,
            dst_ref=dst,
            send_sem=sends.at[slot],
            recv_sem=recvs.at[slot],
            device_id=neighbour(axis, sign),
            device_id_type=MESH,
        )
        copy.start()
        return copy

    for phase in range(axes):
        ones = []
        for p in range(count):
            if phase == 0:
                produce(p)
            axis, reduced = orders[p][phase], orders[p][:phase]
            pair = []
            for k, sign in enumerate((1, -1)):
                start, width = halves(*parts[p])[k]
                far = place(reduced, axis, (at[axis] + 2) % 4) + (slice(None), pl.ds(start, width))
                pair.append(
                    push(
                        buf.at[far], landing(half_in, phase, p, k, width),
                        (phase * count + p) * 4 + k, axis, sign,
                    )
                )
            ones.append(pair)
        twos = []
        for p in range(count):
            axis, reduced = orders[p][phase], orders[p][:phase]
            pair = []
            for k, sign in enumerate((1, -1)):
                ones[p][k].wait_recv()
                start, width = halves(*parts[p])[k]
                near = place(reduced, axis, (at[axis] + sign + 4) % 4)
                half = near + (slice(None), pl.ds(start, width))
                buf[half] = (
                    buf[half].astype(F32) + landing(half_in, phase, p, k, width)[...].astype(F32)
                ).astype(BF16)
                whole = near + (slice(None), pl.ds(*parts[p]))
                pair.append(
                    push(
                        buf.at[whole], landing(full_in, phase, p, k, parts[p][1]),
                        (phase * count + p) * 4 + 2 + k, axis, sign,
                    )
                )
            twos.append(pair)
        for p in range(count):
            axis, reduced = orders[p][phase], orders[p][:phase]
            for k in range(2):
                ones[p][k].wait_send()
                twos[p][k].wait()
            start, width = parts[p]
            own = place(reduced, axis, at[axis]) + (slice(None), pl.ds(start, width))
            total = (
                buf[own].astype(F32)
                + landing(full_in, phase, p, 0, width)[...].astype(F32)
                + landing(full_in, phase, p, 1, width)[...].astype(F32)
            )
            if phase < axes - 1:
                buf[own] = total.astype(BF16)
            else:
                finish(p, pl.ds(start, width), total)


PROJ_PARTS = ((0, 3584), (3584, 3584))


def attention_kernel(
    plan, tab, lens, pool, queries, new_latent, value_up, proj_hbm, resid, gain,
    stream_out, normed_out,
    outgoing, middle, near_fwd, far_fwd, arrived, keys, fresh, lat_send, lat_recv, proj, part,
    wide_sum, h0l, h0r, f0l, f0r, h1l, h1r, f1l, f1r,
    mig_s, mig_r, lat_s, lat_r, part_s, part_r, local_sem,
):
    groups = 16
    me = lax.axis_index("dp")
    lane = lax.axis_index("tp")
    at = (me // 4, me % 4)
    model = proj_hbm.shape[1]

    proj_copy = pltpu.make_async_copy(proj_hbm, proj, local_sem.at[0])
    proj_copy.start()

    def neighbour(axis, sign):
        new = list(at)
        new[axis] = (at[axis] + sign + 4) % 4
        return (new[0] * 4 + new[1], lane)

    barrier = pltpu.get_barrier_semaphore()
    for shift in range(1, groups):
        pl.semaphore_signal(
            barrier, inc=1, device_id=(lax.rem(me + shift, groups), lane), device_id_type=MESH
        )

    for c in range(2):
        def pick(i, carry):
            outgoing[c, i // 4, i % 4] = pool[jnp.maximum(plan[0, i, c], 0)]
            return carry

        lax.fori_loop(0, groups, pick, 0)
    for k in range(2):
        fresh[k] = new_latent[k].astype(F32)
    pl.semaphore_wait(barrier, groups - 1)

    def push(src, dst, slot, axis, sign):
        copy = pltpu.make_async_remote_copy(
            src_ref=src,
            dst_ref=dst,
            send_sem=mig_s.at[slot],
            recv_sem=mig_r.at[slot],
            device_id=neighbour(axis, sign),
            device_id_type=MESH,
        )
        copy.start()
        return copy

    def pair_at(axis, value, k):
        rest = pl.ds(0, 4) if k is None else pl.ds(2 * k, 2)
        return (rest, value) if axis == 1 else (value, rest)

    def local(src, dst, n):
        copy = pltpu.make_async_copy(src, dst, local_sem.at[n])
        copy.start()
        return copy

    for stage in range(2):
        source, target = (outgoing, middle) if stage == 0 else (middle, arrived)
        fwd = (near_fwd, far_fwd)[stage]
        first, kept = [], []
        for c in range(2):
            axis = 1 - c if stage == 0 else c
            far = (at[axis] + 2) % 4
            for k, sign in enumerate((1, -1)):
                base = ((stage * 2 + c) * 2 + k) * 3
                halfway = push(
                    source.at[(c,) + pair_at(axis, far, k)], fwd.at[c, k], base, axis, sign
                )
                beside = push(
                    source.at[(c,) + pair_at(axis, (at[axis] + sign + 4) % 4, None)],
                    target.at[(c,) + pair_at(axis, at[axis], None)],
                    base + 1, axis, sign,
                )
                first.append((c, k, sign, axis, base, halfway, beside))
            own = (c,) + pair_at(axis, at[axis], None)
            kept.append(local(source.at[own], target.at[own], 1 + stage * 2 + c))
        second = []
        for c, k, sign, axis, base, halfway, beside in first:
            halfway.wait_recv()
            came = (at[axis] - sign + 4) % 4
            second.append(
                push(fwd.at[c, k], target.at[(c,) + pair_at(axis, came, k)], base + 2, axis, sign)
            )
        for c, k, sign, axis, base, halfway, beside in first:
            halfway.wait_send()
            beside.wait()
        for copy in second + kept:
            copy.wait()

    def exchange(src, dst, send_sem, recv_sem, shift):
        peer = lax.rem(me + shift, groups)
        return pltpu.make_async_remote_copy(
            src_ref=src(peer),
            dst_ref=dst(me),
            send_sem=send_sem.at[shift - 1],
            recv_sem=recv_sem.at[shift - 1],
            device_id=(peer, lane),
            device_id_type=MESH,
        )

    row = lax.broadcasted_iota(jnp.int32, (128, 128), 0)
    col = lax.broadcasted_iota(jnp.int32, (128, 128), 1)
    reorder = jnp.where(
        col == ((row >> 2) & 1) * 64 + (row >> 3) * 4 + (row & 3), 1.0, 0.0
    ).astype(BF16)
    second_step = ((lax.broadcasted_iota(jnp.int32, (128, 1), 0) >> 2) & 1) == 1
    position = lax.broadcasted_iota(jnp.int32, (128, 1024), 1)

    def attend(s, carry):
        for j in range(8):
            entry = tab[s, j]
            own = pool[jnp.minimum(entry, 23)]
            came = jnp.maximum(entry - 24, 0)
            moved = arrived[came & 1, came >> 3, (came >> 1) & 3]
            keys[:, j * 128:(j + 1) * 128] = jnp.where(entry < 24, own, moved)
        q = jnp.concatenate([queries[0, s], queries[1, s]], axis=0)
        q = dot(reorder, q)
        q16 = q.astype(BF16)
        scores = dot(q16, keys[...]) * SCALE
        scores = jnp.where(position < lens[s], scores, -jnp.inf)
        new0 = fresh[0, pl.ds(s, 1), :]
        new1 = fresh[1, pl.ds(s, 1), :]
        first = jnp.sum(q * new0, axis=1, keepdims=True) * SCALE
        second = jnp.sum(q * new1, axis=1, keepdims=True) * SCALE
        second = jnp.where(second_step, second, -jnp.inf)
        largest = jnp.maximum(jnp.max(scores, axis=1, keepdims=True), jnp.maximum(first, second))
        weights = jnp.exp(scores - largest)
        first = jnp.exp(first - largest)
        second = jnp.exp(second - largest)
        total = jnp.sum(weights, axis=1, keepdims=True) + first + second
        probs = (weights / total).astype(BF16)
        first = (first / total).astype(BF16).astype(F32)
        second = (second / total).astype(BF16).astype(F32)
        latent = dot_nt(probs, keys[0:LAT, :])
        latent = latent + first * new0[:, 0:LAT] + second * new1[:, 0:LAT]
        lat_send[:, pl.ds(s, 1)] = latent.reshape(16, 1, 8, LAT).astype(BF16)
        return carry

    lax.fori_loop(0, 4, attend, 0)

    moves = [
        exchange(lambda p: lat_send.at[p], lambda m: lat_recv.at[m], lat_s, lat_r, shift)
        for shift in range(1, groups)
    ]
    for move in moves:
        move.start()
    lat_recv[me] = lat_send[me]
    for move in moves:
        move.wait()

    rows = lat_recv[...].astype(F32).reshape(512, LAT).astype(BF16)
    row = lax.broadcasted_iota(jnp.int32, (128, 512), 0)
    col = lax.broadcasted_iota(jnp.int32, (128, 512), 1)
    base = (row >> 3) * 32 + (row & 3) * 8 + ((row >> 2) & 1) * 4
    heads = []
    for h in range(4):
        up = dot(rows, value_up[h]).astype(BF16)
        take = jnp.where(col == base + h, 1.0, 0.0).astype(BF16)
        heads.append(dot(take, up).astype(BF16))
    heads = jnp.concatenate(heads, axis=1)
    proj_copy.wait()

    def produce(p):
        start, width = PROJ_PARTS[p]
        chunk = 896
        for n in range(width // chunk):
            cols = pl.ds(start + n * chunk, chunk)
            part[:, :, :, cols] = dot(heads, proj[:, cols]).reshape(4, 4, 8, chunk).astype(BF16)

    def finish(p, cols, total):
        wide_sum[:, cols] = total

    ring_sum(
        at, ((1, 0), (0, 1)), PROJ_PARTS, part, ((h0l, h0r), (h1l, h1r)),
        ((f0l, f0r), (f1l, f1r)), part_s, part_r, neighbour, produce, finish,
    )

    chunk = 1024
    square = jnp.zeros((8, 1), F32)
    for n in range(model // chunk):
        cols = pl.ds(n * chunk, chunk)
        total = wide_sum[:, cols] + jnp.concatenate(
            [resid[0, :, cols].astype(F32), resid[1, :, cols].astype(F32)], axis=0
        )
        stream = total.astype(BF16)
        stream_out[:, cols] = stream
        wide = stream.astype(F32)
        square = square + jnp.sum(wide * wide, axis=1, keepdims=True)
    scale = lax.rsqrt(square * (1.0 / model) + EPS)
    for n in range(model // chunk):
        cols = pl.ds(n * chunk, chunk)
        wide = stream_out[:, cols].astype(F32)
        normed_out[:, cols] = (wide * scale * gain[:, cols]).astype(BF16)


PARTS = ((0, 2432), (2432, 2432), (4864, 2432))
OUT_PARTS = ((0, 2432), (2432, 2432), (4864, 2304))
ROW = 7296


def expert_kernel(
    normed, mix, stream, gate, up, down,
    out,
    rows_buf, rows, hid_w, down_w, acc, obuf,
    h0l, h0r, f0l, f0r, h1l, h1r, f1l, f1r, h2l, h2r, f2l, f2r,
    ag_send, ag_recv, rs_send, rs_recv, w_send, w_recv, w_local,
):
    dp = lax.axis_index("dp")
    tp = lax.axis_index("tp")
    at = (dp // 4, dp % 4, tp // 2)
    core = tp % 2

    def neighbour(axis, sign):
        new = list(at)
        new[axis] = (at[axis] + sign + 4) % 4
        return (new[0] * 4 + new[1], new[2] * 2 + core)

    partner = (dp, (tp // 2) * 2 + (1 - core))

    barrier = pltpu.get_barrier_semaphore()
    for axis in range(3):
        for sign in (1, -1):
            pl.semaphore_signal(
                barrier, inc=1, device_id=neighbour(axis, sign), device_id_type=MESH
            )
    pl.semaphore_signal(barrier, inc=1, device_id=partner, device_id_type=MESH)

    rows_buf[at[0], at[1], at[2], :, 0:7168] = normed[...]
    rows_buf[at[0], at[1], at[2], :, 7168:7296] = mix[...]
    local = []
    remote = []

    def spots(e, which):
        if which < 2:
            base = e * 512 + which * 256
            return (
                hid_w.at[:, pl.ds(base, 128)],
                hid_w.at[:, pl.ds(base + 128, 128)],
            )
        return (
            down_w.at[pl.ds(e * 256, 128)],
            down_w.at[pl.ds(e * 256 + 128, 128)],
        )

    for e in range(2):
        for which, ref in enumerate((gate, up, down)):
            mine, theirs = spots(e, which)
            n = e * 3 + which
            local.append(pltpu.make_async_copy(ref.at[e], mine, w_local.at[n]))
            remote.append(
                pltpu.make_async_remote_copy(
                    src_ref=ref.at[e],
                    dst_ref=theirs,
                    send_sem=w_send.at[n],
                    recv_sem=w_recv.at[n],
                    device_id=partner,
                    device_id_type=MESH,
                )
            )
    for copy in local:
        copy.start()
    pl.semaphore_wait(barrier, 7)

    order = [(p, (p + 1) % 3, (p + 2) % 3) for p in range(3)]

    def place(known, axis, value):
        where = [at[0], at[1], at[2]]
        for a in known:
            where[a] = slice(None)
        where[axis] = value
        return tuple(where)

    def push(ref, dst, sends, recvs, slot, axis, sign):
        return pltpu.make_async_remote_copy(
            src_ref=ref,
            dst_ref=dst,
            send_sem=sends.at[slot],
            recv_sem=recvs.at[slot],
            device_id=neighbour(axis, sign),
            device_id_type=MESH,
        )

    for phase in range(3):
        ones = []
        for p in range(3):
            axis = order[p][phase]
            known = order[p][:phase]
            start, width = PARTS[p]
            own = place(known, axis, at[axis]) + (slice(None), pl.ds(start, width))
            slot = (phase * 3 + p) * 4
            pair = [
                push(rows_buf.at[own], rows_buf.at[own], ag_send, ag_recv, slot + k, axis, sign)
                for k, sign in enumerate((1, -1))
            ]
            for copy in pair:
                copy.start()
            ones.append(pair)
        if phase == 0:
            for copy in remote:
                copy.start()
        twos = []
        for p in range(3):
            axis = order[p][phase]
            known = order[p][:phase]
            slot = (phase * 3 + p) * 4 + 2
            pair = []
            for k, sign in enumerate((1, -1)):
                ones[p][k].wait_recv()
                start, width = halves(*PARTS[p])[k]
                came = place(known, axis, (at[axis] - sign + 4) % 4) + (
                    slice(None), pl.ds(start, width),
                )
                copy = push(
                    rows_buf.at[came], rows_buf.at[came], ag_send, ag_recv, slot + k, axis, sign
                )
                copy.start()
                pair.append(copy)
            twos.append(pair)
        for p in range(3):
            for k in range(2):
                ones[p][k].wait_send()
                twos[p][k].wait()

    for copy in local:
        copy.wait()
    for copy in remote:
        copy.wait()

    for y in range(4):
        rows[pl.ds(y * 128, 128), :] = (
            rows_buf[y].astype(F32).reshape(128, ROW).astype(BF16)
        )
    for n in range(4):
        cols = pl.ds(n * 256, 256)
        acc[:, cols] = dot(rows[:, 0:7168], hid_w[:, cols])
    lanes = lax.broadcasted_iota(jnp.int32, (512, 128), 1)
    table = rows[:, 7168:7296].astype(F32)
    hidden = []
    for e in range(2):
        expert = dp * 2 + e
        mine = (lanes == expert) | (lanes == expert + 32)
        weight = jnp.sum(jnp.where(mine, table, 0.0), axis=1, keepdims=True)
        gate_act = acc[:, e * 512:e * 512 + 256]
        up_act = acc[:, e * 512 + 256:e * 512 + 512]
        hidden.append((gate_act / (1.0 + jnp.exp(-gate_act)) * up_act * weight).astype(BF16))
    hidden = jnp.concatenate(hidden, axis=1)

    def produce(p):
        start, width = OUT_PARTS[p]
        done = 0
        while done < width:
            size = min(256, width - done)
            cols = pl.ds(start + done, size)
            obuf[:, :, :, :, cols] = (
                dot(hidden, down_w[:, cols]).reshape(4, 4, 4, 8, size).astype(BF16)
            )
            done += size

    def finish(p, cols, total):
        total = total + stream[:, cols].astype(F32)
        out[0, :, cols] = total[0:4].astype(BF16)
        out[1, :, cols] = total[4:8].astype(BF16)

    ring_sum(
        at, [o[::-1] for o in order], OUT_PARTS, obuf, ((h0l, h0r), (h1l, h1r), (h2l, h2r)),
        ((f0l, f0r), (f1l, f1r), (f2l, f2r)), rs_send, rs_recv, neighbour, produce, finish,
    )


def per_device(
    cache_pool, send_plan, tables, lengths, new_latent, queries, value_up, out_proj, residual,
    norm_gain, routes, route_weight, gate_proj, up_proj, down_proj,
):
    model = residual.shape[2]
    vmem = pl.BlockSpec(memory_space=pltpu.VMEM)
    smem = pl.BlockSpec(memory_space=pltpu.SMEM)
    hbm = pl.BlockSpec(memory_space=pl.ANY)
    dma = pltpu.SemaphoreType.DMA


    def rings(parts, shape, width):
        return [pltpu.VMEM((parts,) + shape + (8, width), BF16)] * 2

    scratch = [
        pltpu.VMEM((2, 4, 4, 576, 128), BF16),
        pltpu.VMEM((2, 4, 4, 576, 128), BF16),
        pltpu.VMEM((2, 2, 2, 576, 128), BF16),
        pltpu.VMEM((2, 2, 2, 576, 128), BF16),
        pltpu.VMEM((2, 4, 4, 576, 128), BF16),
        pltpu.VMEM((576, 1024), BF16),
        pltpu.VMEM((2, 4, 576), F32),
        pltpu.VMEM((16, 4, 8, LAT), BF16),
        pltpu.VMEM((16, 4, 8, LAT), BF16),
        pltpu.VMEM((512, model), BF16),
        pltpu.VMEM((4, 4, 8, model), BF16),
        pltpu.VMEM((8, model), F32),
    ]
    for shape in ((4,), ()):
        scratch += rings(2, shape, 1792)
        scratch += rings(2, shape, 3584)
    scratch += [dma((24,)), dma((24,)), dma((15,)), dma((15,)), dma((16,)), dma((16,)), dma((5,))]
    stream, normed = pl.pallas_call(
        attention_kernel,
        out_shape=(
            jax.ShapeDtypeStruct((8, model), BF16),
            jax.ShapeDtypeStruct((8, model), BF16),
        ),
        in_specs=[smem, smem, smem, vmem, vmem, vmem, vmem, hbm, vmem, vmem],
        out_specs=(vmem, vmem),
        scratch_shapes=scratch,
        compiler_params=pltpu.CompilerParams(
            collective_id=0, has_side_effects=True, vmem_limit_bytes=56 * MIB
        ),
        name="attention",
    )(
        send_plan, tables, lengths, cache_pool, queries, new_latent, value_up,
        out_proj, residual, norm_gain.reshape(1, model),
    )

    matches = routes.reshape(8, 8)[:, :, None] == jnp.arange(32, dtype=jnp.int32)[None, None, :]
    dense = jnp.sum(jnp.where(matches, route_weight.reshape(8, 8)[:, :, None], 0.0), axis=1)
    high = lax.reduce_precision(dense, 8, 7)
    mix = jnp.concatenate([high, dense - high, jnp.zeros((8, 64), F32)], axis=1).astype(BF16)

    scratch = [
        pltpu.VMEM((4, 4, 4, 8, ROW), BF16),
        pltpu.VMEM((512, ROW), BF16),
        pltpu.VMEM((model, 1024), BF16),
        pltpu.VMEM((512, model), BF16),
        pltpu.VMEM((512, 1024), F32),
        pltpu.VMEM((4, 4, 4, 8, model), BF16),
    ]
    for shape in ((4, 4), (4,), ()):
        scratch += rings(3, shape, 1280)
        scratch += rings(3, shape, 2432)
    scratch += [dma((36,)), dma((36,)), dma((36,)), dma((36,)), dma((6,)), dma((6,)), dma((6,))]
    result = pl.pallas_call(
        expert_kernel,
        out_shape=jax.ShapeDtypeStruct(residual.shape, BF16),
        in_specs=[vmem, vmem, vmem, hbm, hbm, hbm],
        out_specs=vmem,
        scratch_shapes=scratch,
        compiler_params=pltpu.CompilerParams(
            collective_id=1, has_side_effects=True, vmem_limit_bytes=60 * MIB
        ),
        name="experts",
    )(normed, mix, stream, gate_proj, up_proj, down_proj)
    return result


def solution(mesh):
    placed = (
        P(("dp", "tp"), None, None),
        P(("dp", "tp"), None, None),
        P(("dp", "tp"), None),
        P(("dp", "tp")),
        P(None, ("dp", "tp"), None),
        P(None, ("dp", "tp"), None, None),
        P("dp", None, None),
        P("dp", None),
        P(None, ("dp", "tp"), None),
        P(),
        P(None, ("dp", "tp"), None),
        P(None, ("dp", "tp"), None),
        P("dp", None, "tp"),
        P("dp", None, "tp"),
        P("dp", "tp", None),
    )
    return jax.shard_map(
        per_device,
        mesh=mesh,
        in_specs=placed,
        out_specs=P(None, ("dp", "tp"), None),
        check_vma=False,
    )
```

```python
import functools

import jax
import jax.numpy as jnp
from jax import lax
from jax.experimental import pallas as pl
from jax.experimental.pallas import tpu as pltpu
from jax.sharding import PartitionSpec as P

MESH = pl.DeviceIdType.MESH
F32 = jnp.float32
BF16 = jnp.bfloat16
LAT = 512
SCALE = 1.0 / 13.856406460551018
EPS = 1e-06
MIB = 1 << 20


def dot(a, b):
    return jnp.dot(a, b, preferred_element_type=F32)


def dot_nt(a, b):
    return lax.dot_general(a, b, (((1,), (1,)), ((), ())), preferred_element_type=F32)


def halves(start, width):
    tiles = width // 128
    first = (tiles + 1) // 2 * 128
    return (start, first), (start + first, width - first)


def ring_sum(at, orders, parts, buf, half_in, full_in, sends, recvs, neighbour, produce, finish):
    axes = len(orders[0])
    count = len(parts)

    def place(reduced, axis, value):
        where = [slice(None)] * axes
        for a in reduced:
            where[a] = at[a]
        where[axis] = value
        return tuple(where)

    def landing(refs, phase, p, k, width):
        return refs[phase][k].at[(p,) + (slice(None),) * (axes - phase) + (pl.ds(0, width),)]

    def push(src, dst, slot, axis, sign):
        copy = pltpu.make_async_remote_copy(
            src_ref=src,
            dst_ref=dst,
            send_sem=sends.at[slot],
            recv_sem=recvs.at[slot],
            device_id=neighbour(axis, sign),
            device_id_type=MESH,
        )
        copy.start()
        return copy

    for phase in range(axes):
        ones = []
        for p in range(count):
            if phase == 0:
                produce(p)
            axis, reduced = orders[p][phase], orders[p][:phase]
            pair = []
            for k, sign in enumerate((1, -1)):
                start, width = halves(*parts[p])[k]
                far = place(reduced, axis, (at[axis] + 2) % 4) + (slice(None), pl.ds(start, width))
                pair.append(
                    push(
                        buf.at[far], landing(half_in, phase, p, k, width),
                        (phase * count + p) * 4 + k, axis, sign,
                    )
                )
            ones.append(pair)
        twos = []
        for p in range(count):
            axis, reduced = orders[p][phase], orders[p][:phase]
            pair = []
            for k, sign in enumerate((1, -1)):
                ones[p][k].wait_recv()
                start, width = halves(*parts[p])[k]
                near = place(reduced, axis, (at[axis] + sign + 4) % 4)
                half = near + (slice(None), pl.ds(start, width))
                buf[half] = (
                    buf[half].astype(F32) + landing(half_in, phase, p, k, width)[...].astype(F32)
                ).astype(BF16)
                whole = near + (slice(None), pl.ds(*parts[p]))
                pair.append(
                    push(
                        buf.at[whole], landing(full_in, phase, p, k, parts[p][1]),
                        (phase * count + p) * 4 + 2 + k, axis, sign,
                    )
                )
            twos.append(pair)
        for p in range(count):
            axis, reduced = orders[p][phase], orders[p][:phase]
            for k in range(2):
                ones[p][k].wait_send()
                twos[p][k].wait()
            start, width = parts[p]
            own = place(reduced, axis, at[axis]) + (slice(None), pl.ds(start, width))
            total = (
                buf[own].astype(F32)
                + landing(full_in, phase, p, 0, width)[...].astype(F32)
                + landing(full_in, phase, p, 1, width)[...].astype(F32)
            )
            if phase < axes - 1:
                buf[own] = total.astype(BF16)
            else:
                finish(p, pl.ds(start, width), total)


PROJ_PARTS = ((0, 3584), (3584, 3584))


def attention_kernel(
    plan, tab, lens, pool, queries, new_latent, value_up, proj_hbm, resid, gain,
    stream_out, normed_out,
    outgoing, middle, near_fwd, far_fwd, arrived, keys, fresh, lat_send, lat_recv, proj, part,
    wide_sum, h0l, h0r, f0l, f0r, h1l, h1r, f1l, f1r,
    mig_s, mig_r, lat_s, lat_r, part_s, part_r, local_sem,
):
    groups = 16
    me = lax.axis_index("dp")
    lane = lax.axis_index("tp")
    at = (me // 4, me % 4)
    model = proj_hbm.shape[1]

    proj_copy = pltpu.make_async_copy(proj_hbm, proj, local_sem.at[0])
    proj_copy.start()

    def neighbour(axis, sign):
        new = list(at)
        new[axis] = (at[axis] + sign + 4) % 4
        return (new[0] * 4 + new[1], lane)

    barrier = pltpu.get_barrier_semaphore()
    for shift in range(1, groups):
        pl.semaphore_signal(
            barrier, inc=1, device_id=(lax.rem(me + shift, groups), lane), device_id_type=MESH
        )

    for c in range(2):
        def pick(i, carry):
            outgoing[c, i // 4, i % 4] = pool[jnp.maximum(plan[0, i, c], 0)]
            return carry

        lax.fori_loop(0, groups, pick, 0)
    for k in range(2):
        fresh[k] = new_latent[k].astype(F32)
    pl.semaphore_wait(barrier, groups - 1)

    def push(src, dst, slot, axis, sign):
        copy = pltpu.make_async_remote_copy(
            src_ref=src,
            dst_ref=dst,
            send_sem=mig_s.at[slot],
            recv_sem=mig_r.at[slot],
            device_id=neighbour(axis, sign),
            device_id_type=MESH,
        )
        copy.start()
        return copy

    def pair_at(axis, value, k):
        rest = pl.ds(0, 4) if k is None else pl.ds(2 * k, 2)
        return (rest, value) if axis == 1 else (value, rest)

    def local(src, dst, n):
        copy = pltpu.make_async_copy(src, dst, local_sem.at[n])
        copy.start()
        return copy

    for stage in range(2):
        source, target = (outgoing, middle) if stage == 0 else (middle, arrived)
        fwd = (near_fwd, far_fwd)[stage]
        first, kept = [], []
        for c in range(2):
            axis = 1 - c if stage == 0 else c
            far = (at[axis] + 2) % 4
            for k, sign in enumerate((1, -1)):
                base = ((stage * 2 + c) * 2 + k) * 3
                halfway = push(
                    source.at[(c,) + pair_at(axis, far, k)], fwd.at[c, k], base, axis, sign
                )
                beside = push(
                    source.at[(c,) + pair_at(axis, (at[axis] + sign + 4) % 4, None)],
                    target.at[(c,) + pair_at(axis, at[axis], None)],
                    base + 1, axis, sign,
                )
                first.append((c, k, sign, axis, base, halfway, beside))
            own = (c,) + pair_at(axis, at[axis], None)
            kept.append(local(source.at[own], target.at[own], 1 + stage * 2 + c))
        second = []
        for c, k, sign, axis, base, halfway, beside in first:
            halfway.wait_recv()
            came = (at[axis] - sign + 4) % 4
            second.append(
                push(fwd.at[c, k], target.at[(c,) + pair_at(axis, came, k)], base + 2, axis, sign)
            )
        for c, k, sign, axis, base, halfway, beside in first:
            halfway.wait_send()
            beside.wait()
        for copy in second + kept:
            copy.wait()

    def exchange(src, dst, send_sem, recv_sem, shift):
        peer = lax.rem(me + shift, groups)
        return pltpu.make_async_remote_copy(
            src_ref=src(peer),
            dst_ref=dst(me),
            send_sem=send_sem.at[shift - 1],
            recv_sem=recv_sem.at[shift - 1],
            device_id=(peer, lane),
            device_id_type=MESH,
        )

    row = lax.broadcasted_iota(jnp.int32, (128, 128), 0)
    col = lax.broadcasted_iota(jnp.int32, (128, 128), 1)
    reorder = jnp.where(
        col == ((row >> 2) & 1) * 64 + (row >> 3) * 4 + (row & 3), 1.0, 0.0
    ).astype(BF16)
    second_step = ((lax.broadcasted_iota(jnp.int32, (128, 1), 0) >> 2) & 1) == 1
    position = lax.broadcasted_iota(jnp.int32, (128, 1024), 1)

    def attend(s, carry):
        for j in range(8):
            entry = tab[s, j]
            own = pool[jnp.minimum(entry, 23)]
            came = jnp.maximum(entry - 24, 0)
            moved = arrived[came & 1, came >> 3, (came >> 1) & 3]
            keys[:, j * 128:(j + 1) * 128] = jnp.where(entry < 24, own, moved)
        q = jnp.concatenate([queries[0, s], queries[1, s]], axis=0)
        q = dot(reorder, q)
        q16 = q.astype(BF16)
        scores = dot(q16, keys[...]) * SCALE
        scores = jnp.where(position < lens[s], scores, -jnp.inf)
        new0 = fresh[0, pl.ds(s, 1), :]
        new1 = fresh[1, pl.ds(s, 1), :]
        first = jnp.sum(q * new0, axis=1, keepdims=True) * SCALE
        second = jnp.sum(q * new1, axis=1, keepdims=True) * SCALE
        second = jnp.where(second_step, second, -jnp.inf)
        largest = jnp.maximum(jnp.max(scores, axis=1, keepdims=True), jnp.maximum(first, second))
        weights = jnp.exp(scores - largest)
        first = jnp.exp(first - largest)
        second = jnp.exp(second - largest)
        total = jnp.sum(weights, axis=1, keepdims=True) + first + second
        probs = (weights / total).astype(BF16)
        first = (first / total).astype(BF16).astype(F32)
        second = (second / total).astype(BF16).astype(F32)
        latent = dot_nt(probs, keys[0:LAT, :])
        latent = latent + first * new0[:, 0:LAT] + second * new1[:, 0:LAT]
        lat_send[:, pl.ds(s, 1)] = latent.reshape(16, 1, 8, LAT).astype(BF16)
        return carry

    lax.fori_loop(0, 4, attend, 0)

    moves = [
        exchange(lambda p: lat_send.at[p], lambda m: lat_recv.at[m], lat_s, lat_r, shift)
        for shift in range(1, groups)
    ]
    for move in moves:
        move.start()
    lat_recv[me] = lat_send[me]
    for move in moves:
        move.wait()

    rows = lat_recv[...].astype(F32).reshape(512, LAT).astype(BF16)
    row = lax.broadcasted_iota(jnp.int32, (128, 512), 0)
    col = lax.broadcasted_iota(jnp.int32, (128, 512), 1)
    base = (row >> 3) * 32 + (row & 3) * 8 + ((row >> 2) & 1) * 4
    heads = []
    for h in range(4):
        up = dot(rows, value_up[h]).astype(BF16)
        take = jnp.where(col == base + h, 1.0, 0.0).astype(BF16)
        heads.append(dot(take, up).astype(BF16))
    heads = jnp.concatenate(heads, axis=1)
    proj_copy.wait()

    def produce(p):
        start, width = PROJ_PARTS[p]
        chunk = 896
        for n in range(width // chunk):
            cols = pl.ds(start + n * chunk, chunk)
            part[:, :, :, cols] = dot(heads, proj[:, cols]).reshape(4, 4, 8, chunk).astype(BF16)

    def finish(p, cols, total):
        wide_sum[:, cols] = total

    ring_sum(
        at, ((1, 0), (0, 1)), PROJ_PARTS, part, ((h0l, h0r), (h1l, h1r)),
        ((f0l, f0r), (f1l, f1r)), part_s, part_r, neighbour, produce, finish,
    )

    chunk = 1024
    square = jnp.zeros((8, 1), F32)
    for n in range(model // chunk):
        cols = pl.ds(n * chunk, chunk)
        total = wide_sum[:, cols] + jnp.concatenate(
            [resid[0, :, cols].astype(F32), resid[1, :, cols].astype(F32)], axis=0
        )
        stream = total.astype(BF16)
        stream_out[:, cols] = stream
        wide = stream.astype(F32)
        square = square + jnp.sum(wide * wide, axis=1, keepdims=True)
    scale = lax.rsqrt(square * (1.0 / model) + EPS)
    for n in range(model // chunk):
        cols = pl.ds(n * chunk, chunk)
        wide = stream_out[:, cols].astype(F32)
        normed_out[:, cols] = (wide * scale * gain[:, cols]).astype(BF16)


PARTS = ((0, 2432), (2432, 2432), (4864, 2432))
OUT_PARTS = ((0, 2432), (2432, 2432), (4864, 2304))
ROW = 7296


def expert_kernel(
    normed, mix, stream, gate, up, down,
    out,
    rows, hid_w, down_w, acc, obuf,
    h0l, h0r, f0l, f0r, h1l, h1r, f1l, f1r, h2l, h2r, f2l, f2r,
    g0_send, g0_recv, g1_send, g1_recv, g2_send, g2_recv,
    s0_send, s0_recv, s1_send, s1_recv, s2_send, s2_recv, w_send, w_recv, w_local,
):
    dp = lax.axis_index("dp")
    tp = lax.axis_index("tp")
    at = (dp // 4, dp % 4, tp // 2)
    core = tp % 2
    signs = (1, -1)
    every = slice(None)

    def neighbour(axis, sign):
        new = list(at)
        new[axis] = (at[axis] + sign + 4) % 4
        return (new[0] * 4 + new[1], new[2] * 2 + core)

    partner = (dp, (tp // 2) * 2 + (1 - core))

    barrier = pltpu.get_barrier_semaphore()
    for axis in range(3):
        for sign in signs:
            pl.semaphore_signal(
                barrier, inc=1, device_id=neighbour(axis, sign), device_id_type=MESH
            )
    pl.semaphore_signal(barrier, inc=1, device_id=partner, device_id_type=MESH)

    rows[at[0], at[1], at[2], :, 0:7168] = normed[...]
    rows[at[0], at[1], at[2], :, 7168:7296] = mix[...]
    local = []
    remote = []

    def spots(e, which):
        if which < 2:
            base = e * 512 + which * 256
            return hid_w.at[:, pl.ds(base, 128)], hid_w.at[:, pl.ds(base + 128, 128)]
        return down_w.at[pl.ds(e * 256, 128)], down_w.at[pl.ds(e * 256 + 128, 128)]

    for e in range(2):
        for which, ref in enumerate((gate, up, down)):
            mine, theirs = spots(e, which)
            n = e * 3 + which
            local.append(pltpu.make_async_copy(ref.at[e], mine, w_local.at[n]))
            remote.append(
                pltpu.make_async_remote_copy(
                    src_ref=ref.at[e],
                    dst_ref=theirs,
                    send_sem=w_send.at[n],
                    recv_sem=w_recv.at[n],
                    device_id=partner,
                    device_id_type=MESH,
                )
            )
    for copy in local:
        copy.start()
    pl.semaphore_wait(barrier, 7)

    order = [(p, (p + 1) % 3, (p + 2) % 3) for p in range(3)]

    def shifted(axis, offset):
        return (at[axis] + offset + 4) % 4

    def block(p, values, start, width):
        where = [None] * 3
        for axis, value in zip(order[p], values):
            where[axis] = every if value is None else value
        return tuple(where) + (every, pl.ds(start, width))

    def push(src, dst, sends, recvs, slot, axis, sign):
        copy = pltpu.make_async_remote_copy(
            src_ref=src,
            dst_ref=dst,
            send_sem=sends.at[slot],
            recv_sem=recvs.at[slot],
            device_id=neighbour(axis, sign),
            device_id_type=MESH,
        )
        copy.start()
        return copy

    def both(p, values, axis, sems, slot):
        ref = rows.at[block(p, values, *PARTS[p])]
        return [push(ref, ref, *sems, slot + k, axis, sign) for k, sign in enumerate(signs)]

    def forward(p, k, came, axis, sems, slot):
        ref = rows.at[block(p, came, *halves(*PARTS[p])[k])]
        return push(ref, ref, *sems, slot + 2 + k, axis, signs[k])

    sems0, sems1, sems2 = (g0_send, g0_recv), (g1_send, g1_recv), (g2_send, g2_recv)
    one, two = {}, {}

    def start_unit(p, d):
        a, b, c = order[p]
        one[2, p, d] = both(p, (None, shifted(b, d), at[c]), c, sems2, (p * 4 + d) * 4)

    def forward_unit(p, d):
        a, b, c = order[p]
        two[2, p, d] = []
        for k in range(2):
            one[2, p, d][k].wait_recv()
            two[2, p, d].append(
                forward(
                    p, k, (None, shifted(b, d), shifted(c, -signs[k])), c, sems2, (p * 4 + d) * 4
                )
            )

    for p in range(3):
        a, b, c = order[p]
        one[0, p] = both(p, (at[a], at[b], at[c]), a, sems0, p * 4)
    for copy in remote:
        copy.start()
    for p in range(3):
        a, b, c = order[p]
        two[0, p] = []
        for k in range(2):
            one[0, p][k].wait_recv()
            two[0, p].append(
                forward(p, k, (shifted(a, -signs[k]), at[b], at[c]), a, sems0, p * 4)
            )
    for p in range(3):
        a, b, c = order[p]
        for copy in two[0, p]:
            copy.wait_recv()
        one[1, p] = both(p, (None, at[b], at[c]), b, sems1, p * 4)
        start_unit(p, 0)
    for p in range(3):
        a, b, c = order[p]
        two[1, p] = []
        for k in range(2):
            one[1, p][k].wait_recv()
            two[1, p].append(
                forward(p, k, (None, shifted(b, -signs[k]), at[c]), b, sems1, p * 4)
            )
        start_unit(p, 3)
        start_unit(p, 1)
    for p in range(3):
        forward_unit(p, 0)
    for p in range(3):
        for copy in two[1, p]:
            copy.wait_recv()
        start_unit(p, 2)
    for d in (3, 1):
        for p in range(3):
            forward_unit(p, d)

    acc[...] = jnp.zeros_like(acc)
    for copy in local:
        copy.wait()
    for copy in remote:
        copy.wait()

    def multiply(p, d):
        a, b, c = order[p]
        for copy in two[2, p, d]:
            copy.wait_recv()
        start, width = OUT_PARTS[p]
        lhs = rows[block(p, (None, shifted(b, d), None), start, width)]
        lhs = lhs.astype(F32).reshape(128, width).astype(BF16)
        for n in range(4):
            cols = (n * 256, 256)
            where = block(p, (None, shifted(b, d), None), *cols)
            product = dot(lhs, hid_w[pl.ds(start, width), pl.ds(*cols)])
            acc[where] = acc[where] + product.reshape(4, 4, 8, 256)

    for p in range(3):
        multiply(p, 0)
    for p in range(3):
        forward_unit(p, 2)
    for d in (3, 1, 2):
        for p in range(3):
            multiply(p, d)
    for pair in one.values():
        for copy in pair:
            copy.wait_send()
    for pair in two.values():
        for copy in pair:
            copy.wait_send()

    lanes = lax.broadcasted_iota(jnp.int32, (512, 128), 1)
    table = rows[:, :, :, :, 7168:7296].astype(F32).reshape(512, 128)
    hidden = []
    for e in range(2):
        expert = dp * 2 + e
        mine = (lanes == expert) | (lanes == expert + 32)
        weight = jnp.sum(jnp.where(mine, table, 0.0), axis=1, keepdims=True)
        gate_act = acc[:, :, :, :, e * 512:e * 512 + 256].reshape(512, 256)
        up_act = acc[:, :, :, :, e * 512 + 256:e * 512 + 512].reshape(512, 256)
        hidden.append((gate_act / (1.0 + jnp.exp(-gate_act)) * up_act * weight).astype(BF16))
    hidden = jnp.concatenate(hidden, axis=1)

    half_in = ((h0l, h0r), (h1l, h1r), (h2l, h2r))
    full_in = ((f0l, f0r), (f1l, f1r), (f2l, f2r))
    sums0, sums1, sums2 = (s0_send, s0_recv), (s1_send, s1_recv), (s2_send, s2_recv)
    sums = (sums0, sums1, sums2)
    far, near, base = {}, {}, {}

    def spot(level, p, d, offset):
        a, b, c = order[p]
        if level == 0:
            return (None, shifted(b, d), shifted(c, offset)), c
        if level == 1:
            return (None, shifted(b, offset), at[c]), b
        return (shifted(a, offset), at[b], at[c]), a

    def landing(refs, level, p, d, k, width):
        lead = (p, d) if level == 0 else (p,)
        return refs[level][k].at[lead + (every,) * (1 if level == 2 else 2) + (pl.ds(0, width),)]

    def send_far(level, p, d):
        slot = ((p * 4 + d) if level == 0 else p) * 4
        far[level, p, d] = []
        for k, sign in enumerate(signs):
            values, axis = spot(level, p, d, 2)
            start, width = halves(*OUT_PARTS[p])[k]
            far[level, p, d].append(
                push(
                    obuf.at[block(p, values, start, width)],
                    landing(half_in, level, p, d, k, width), *sums[level], slot + k, axis, sign,
                )
            )

    def send_near(level, p, d, k):
        slot = ((p * 4 + d) if level == 0 else p) * 4
        far[level, p, d][k].wait_recv()
        values, axis = spot(level, p, d, signs[k])
        start, width = halves(*OUT_PARTS[p])[k]
        half = block(p, values, start, width)
        obuf[half] = (
            obuf[half].astype(F32) + landing(half_in, level, p, d, k, width)[...].astype(F32)
        ).astype(BF16)
        near[level, p, d, k] = push(
            obuf.at[block(p, values, *OUT_PARTS[p])],
            landing(full_in, level, p, d, k, OUT_PARTS[p][1]), *sums[level], slot + 2 + k, axis,
            signs[k],
        )

    def own_sum(level, p, d):
        values, _ = spot(level, p, d, 0)
        where = block(p, values, *OUT_PARTS[p])
        total = obuf[where].astype(F32)
        for k in range(2):
            near[level, p, d, k].wait_recv()
            total = total + landing(full_in, level, p, d, k, OUT_PARTS[p][1])[...].astype(F32)
        if level < 2:
            obuf[where] = total.astype(BF16)
        return total

    for p in range(3):
        start, width = OUT_PARTS[p]
        done = 0
        while done < width:
            size = min(256, width - done)
            cols = pl.ds(start + done, size)
            obuf[:, :, :, :, cols] = (
                dot(hidden, down_w[:, cols]).reshape(4, 4, 4, 8, size).astype(BF16)
            )
            done += size
        for d in (2, 1, 3, 0):
            send_far(0, p, d)
    for d in (2, 1, 3, 0):
        for p in range(3):
            for k in range(2):
                send_near(0, p, d, k)
    for p in range(3):
        own_sum(0, p, 2)
        send_far(1, p, 0)
    for k, d in enumerate((1, 3)):
        for p in range(3):
            own_sum(0, p, d)
            send_near(1, p, 0, k)
    for p in range(3):
        own_sum(0, p, 0)
    for p in range(3):
        own_sum(1, p, 0)
        send_far(2, p, 0)
    for k in range(2):
        for p in range(3):
            send_near(2, p, 0, k)
    for p in range(3):
        total = own_sum(2, p, 0)
        cols = pl.ds(*OUT_PARTS[p])
        total = total + stream[:, cols].astype(F32)
        out[0, :, cols] = total[0:4].astype(BF16)
        out[1, :, cols] = total[4:8].astype(BF16)
    for pair in far.values():
        for copy in pair:
            copy.wait_send()
    for copy in near.values():
        copy.wait_send()


def per_device(
    cache_pool, send_plan, tables, lengths, new_latent, queries, value_up, out_proj, residual,
    norm_gain, routes, route_weight, gate_proj, up_proj, down_proj,
):
    model = residual.shape[2]
    vmem = pl.BlockSpec(memory_space=pltpu.VMEM)
    smem = pl.BlockSpec(memory_space=pltpu.SMEM)
    hbm = pl.BlockSpec(memory_space=pl.ANY)
    dma = pltpu.SemaphoreType.DMA


    def rings(parts, shape, width):
        return [pltpu.VMEM((parts,) + shape + (8, width), BF16)] * 2

    scratch = [
        pltpu.VMEM((2, 4, 4, 576, 128), BF16),
        pltpu.VMEM((2, 4, 4, 576, 128), BF16),
        pltpu.VMEM((2, 2, 2, 576, 128), BF16),
        pltpu.VMEM((2, 2, 2, 576, 128), BF16),
        pltpu.VMEM((2, 4, 4, 576, 128), BF16),
        pltpu.VMEM((576, 1024), BF16),
        pltpu.VMEM((2, 4, 576), F32),
        pltpu.VMEM((16, 4, 8, LAT), BF16),
        pltpu.VMEM((16, 4, 8, LAT), BF16),
        pltpu.VMEM((512, model), BF16),
        pltpu.VMEM((4, 4, 8, model), BF16),
        pltpu.VMEM((8, model), F32),
    ]
    for shape in ((4,), ()):
        scratch += rings(2, shape, 1792)
        scratch += rings(2, shape, 3584)
    scratch += [dma((24,)), dma((24,)), dma((15,)), dma((15,)), dma((16,)), dma((16,)), dma((5,))]
    stream, normed = pl.pallas_call(
        attention_kernel,
        out_shape=(
            jax.ShapeDtypeStruct((8, model), BF16),
            jax.ShapeDtypeStruct((8, model), BF16),
        ),
        in_specs=[smem, smem, smem, vmem, vmem, vmem, vmem, hbm, vmem, vmem],
        out_specs=(vmem, vmem),
        scratch_shapes=scratch,
        compiler_params=pltpu.CompilerParams(
            collective_id=0, has_side_effects=True, vmem_limit_bytes=56 * MIB
        ),
        name="attention",
    )(
        send_plan, tables, lengths, cache_pool, queries, new_latent, value_up,
        out_proj, residual, norm_gain.reshape(1, model),
    )

    matches = routes.reshape(8, 8)[:, :, None] == jnp.arange(32, dtype=jnp.int32)[None, None, :]
    dense = jnp.sum(jnp.where(matches, route_weight.reshape(8, 8)[:, :, None], 0.0), axis=1)
    high = lax.reduce_precision(dense, 8, 7)
    mix = jnp.concatenate([high, dense - high, jnp.zeros((8, 64), F32)], axis=1).astype(BF16)

    scratch = [
        pltpu.VMEM((4, 4, 4, 8, ROW), BF16),
        pltpu.VMEM((model, 1024), BF16),
        pltpu.VMEM((512, model), BF16),
        pltpu.VMEM((4, 4, 4, 8, 1024), F32),
        pltpu.VMEM((4, 4, 4, 8, model), BF16),
    ]
    for shape in ((4, 4), (4,), ()):
        scratch += rings(3, shape, 1280)
        scratch += rings(3, shape, 2432)
    scratch += [dma((n,)) for n in (12, 12, 12, 12, 48, 48, 48, 48, 12, 12, 12, 12, 6, 6, 6)]
    result = pl.pallas_call(
        expert_kernel,
        out_shape=jax.ShapeDtypeStruct(residual.shape, BF16),
        in_specs=[vmem, vmem, vmem, hbm, hbm, hbm],
        out_specs=vmem,
        scratch_shapes=scratch,
        compiler_params=pltpu.CompilerParams(
            collective_id=1, has_side_effects=True, vmem_limit_bytes=60 * MIB
        ),
        name="experts",
    )(normed, mix, stream, gate_proj, up_proj, down_proj)
    return result


def solution(mesh):
    placed = (
        P(("dp", "tp"), None, None),
        P(("dp", "tp"), None, None),
        P(("dp", "tp"), None),
        P(("dp", "tp")),
        P(None, ("dp", "tp"), None),
        P(None, ("dp", "tp"), None, None),
        P("dp", None, None),
        P("dp", None),
        P(None, ("dp", "tp"), None),
        P(),
        P(None, ("dp", "tp"), None),
        P(None, ("dp", "tp"), None),
        P("dp", None, "tp"),
        P("dp", None, "tp"),
        P("dp", "tp", None),
    )
    return jax.shard_map(
        per_device,
        mesh=mesh,
        in_specs=placed,
        out_specs=P(None, ("dp", "tp"), None),
        check_vma=False,
    )
```

```python
import functools

import jax
import jax.numpy as jnp
from jax import lax
from jax.experimental import pallas as pl
from jax.experimental.pallas import tpu as pltpu
from jax.sharding import PartitionSpec as P

MESH = pl.DeviceIdType.MESH
F32 = jnp.float32
BF16 = jnp.bfloat16
LAT = 512
SCALE = 1.0 / 13.856406460551018
EPS = 1e-06
MIB = 1 << 20


def dot(a, b):
    return jnp.dot(a, b, preferred_element_type=F32)


def dot_nt(a, b):
    return lax.dot_general(a, b, (((1,), (1,)), ((), ())), preferred_element_type=F32)


def halves(start, width):
    tiles = width // 128
    first = (tiles + 1) // 2 * 128
    return (start, first), (start + first, width - first)


def ring_sum(
    at, orders, streams, parts, buf, half_in, full_in, sends, recvs, neighbour, produce, finish
):
    axes = len(orders[0])
    count = len(parts)
    signs = (1, -1)
    far, near = {}, {}

    def place(phase, p, offset):
        where = [slice(None)] * axes
        for a in orders[p][:phase]:
            where[a] = at[a]
        axis = orders[p][phase]
        where[axis] = (at[axis] + offset + 4) % 4
        return tuple(where) + (slice(None),)

    def landing(refs, phase, p, k, width):
        return refs[phase][k].at[(p,) + (slice(None),) * (axes - phase) + (pl.ds(0, width),)]

    def push(src, dst, slot, axis, sign):
        copy = pltpu.make_async_remote_copy(
            src_ref=src,
            dst_ref=dst,
            send_sem=sends.at[slot],
            recv_sem=recvs.at[slot],
            device_id=neighbour(axis, sign),
            device_id_type=MESH,
        )
        copy.start()
        return copy

    def send_far(phase, p):
        for k in range(2):
            start, width = halves(*parts[p])[k]
            far[phase, p, k] = push(
                buf.at[place(phase, p, 2) + (pl.ds(start, width),)],
                landing(half_in, phase, p, k, width),
                (phase * count + p) * 4 + k, orders[p][phase], signs[k],
            )

    def send_near(phase, p, k):
        far[phase, p, k].wait_recv()
        start, width = halves(*parts[p])[k]
        half = place(phase, p, signs[k]) + (pl.ds(start, width),)
        buf[half] = (
            buf[half].astype(F32) + landing(half_in, phase, p, k, width)[...].astype(F32)
        ).astype(BF16)
        near[phase, p, k] = push(
            buf.at[place(phase, p, signs[k]) + (pl.ds(*parts[p]),)],
            landing(full_in, phase, p, k, parts[p][1]),
            (phase * count + p) * 4 + 2 + k, orders[p][phase], signs[k],
        )

    def own_sum(phase, p):
        where = place(phase, p, 0) + (pl.ds(*parts[p]),)
        total = buf[where].astype(F32)
        for k in range(2):
            near[phase, p, k].wait_recv()
            total = total + landing(full_in, phase, p, k, parts[p][1])[...].astype(F32)
        if phase < axes - 1:
            buf[where] = total.astype(BF16)
        return total

    for phase in range(axes):
        for stream in streams:
            for p in stream:
                if phase == 0:
                    produce(p)
                else:
                    own_sum(phase - 1, p)
                send_far(phase, p)
        for stream in streams:
            for p in stream:
                for k in range(2):
                    send_near(phase, p, k)
    for stream in streams:
        for p in stream:
            finish(p, pl.ds(*parts[p]), own_sum(axes - 1, p))
    for copy in list(far.values()) + list(near.values()):
        copy.wait_send()


PROJ_PARTS = ((0, 1792), (3584, 1792), (1792, 1792), (5376, 1792))
PROJ_ORDERS = ((1, 0), (0, 1), (1, 0), (0, 1))


def attention_kernel(
    plan, tab, lens, pool, queries, new_latent, value_up, proj_hbm, resid, gain,
    stream_out, normed_out,
    outgoing, middle, near_fwd, far_fwd, arrived, keys, fresh, lat_send, lat_recv, proj, part,
    wide_sum, h0l, h0r, f0l, f0r, h1l, h1r, f1l, f1r,
    mig_s, mig_r, lat_s, lat_r, part_s, part_r, local_sem,
):
    groups = 16
    me = lax.axis_index("dp")
    lane = lax.axis_index("tp")
    at = (me // 4, me % 4)
    model = proj_hbm.shape[1]

    proj_copy = pltpu.make_async_copy(proj_hbm, proj, local_sem.at[0])
    proj_copy.start()

    def neighbour(axis, sign):
        new = list(at)
        new[axis] = (at[axis] + sign + 4) % 4
        return (new[0] * 4 + new[1], lane)

    barrier = pltpu.get_barrier_semaphore()
    for shift in range(1, groups):
        pl.semaphore_signal(
            barrier, inc=1, device_id=(lax.rem(me + shift, groups), lane), device_id_type=MESH
        )

    for c in range(2):
        def pick(i, carry):
            outgoing[c, i // 4, i % 4] = pool[jnp.maximum(plan[0, c, i], 0)]
            return carry

        lax.fori_loop(0, groups, pick, 0)
    for k in range(2):
        fresh[k] = new_latent[k].astype(F32)
    pl.semaphore_wait(barrier, groups - 1)

    def push(src, dst, slot, axis, sign):
        copy = pltpu.make_async_remote_copy(
            src_ref=src,
            dst_ref=dst,
            send_sem=mig_s.at[slot],
            recv_sem=mig_r.at[slot],
            device_id=neighbour(axis, sign),
            device_id_type=MESH,
        )
        copy.start()
        return copy

    def pair_at(axis, value, k):
        rest = pl.ds(0, 4) if k is None else pl.ds(2 * k, 2)
        return (rest, value) if axis == 1 else (value, rest)

    def local(src, dst, n):
        copy = pltpu.make_async_copy(src, dst, local_sem.at[n])
        copy.start()
        return copy

    for stage in range(2):
        source, target = (outgoing, middle) if stage == 0 else (middle, arrived)
        fwd = (near_fwd, far_fwd)[stage]
        first, kept = [], []
        for c in range(2):
            axis = 1 - c if stage == 0 else c
            far = (at[axis] + 2) % 4
            for k, sign in enumerate((1, -1)):
                base = ((stage * 2 + c) * 2 + k) * 3
                halfway = push(
                    source.at[(c,) + pair_at(axis, far, k)], fwd.at[c, k], base, axis, sign
                )
                beside = push(
                    source.at[(c,) + pair_at(axis, (at[axis] + sign + 4) % 4, None)],
                    target.at[(c,) + pair_at(axis, at[axis], None)],
                    base + 1, axis, sign,
                )
                first.append((c, k, sign, axis, base, halfway, beside))
            own = (c,) + pair_at(axis, at[axis], None)
            kept.append(local(source.at[own], target.at[own], 1 + stage * 2 + c))
        second = []
        for c, k, sign, axis, base, halfway, beside in first:
            halfway.wait_recv()
            came = (at[axis] - sign + 4) % 4
            second.append(
                push(fwd.at[c, k], target.at[(c,) + pair_at(axis, came, k)], base + 2, axis, sign)
            )
        for c, k, sign, axis, base, halfway, beside in first:
            halfway.wait_send()
            beside.wait()
        for copy in second + kept:
            copy.wait()

    def exchange(src, dst, send_sem, recv_sem, shift):
        peer = lax.rem(me + shift, groups)
        return pltpu.make_async_remote_copy(
            src_ref=src(peer),
            dst_ref=dst(me),
            send_sem=send_sem.at[shift - 1],
            recv_sem=recv_sem.at[shift - 1],
            device_id=(peer, lane),
            device_id_type=MESH,
        )

    row = lax.broadcasted_iota(jnp.int32, (128, 128), 0)
    col = lax.broadcasted_iota(jnp.int32, (128, 128), 1)
    reorder = jnp.where(
        col == ((row >> 2) & 1) * 64 + (row >> 3) * 4 + (row & 3), 1.0, 0.0
    ).astype(BF16)
    second_step = ((lax.broadcasted_iota(jnp.int32, (128, 1), 0) >> 2) & 1) == 1
    position = lax.broadcasted_iota(jnp.int32, (128, 1024), 1)

    def attend(s, carry):
        for j in range(8):
            entry = tab[s, j]
            own = pool[jnp.minimum(entry, 23)]
            came = jnp.maximum(entry - 24, 0)
            moved = arrived[came & 1, came >> 3, (came >> 1) & 3]
            keys[:, j * 128:(j + 1) * 128] = jnp.where(entry < 24, own, moved)
        q = jnp.concatenate([queries[0, s], queries[1, s]], axis=0)
        q = dot(reorder, q)
        q16 = q.astype(BF16)
        scores = dot(q16, keys[...]) * SCALE
        scores = jnp.where(position < lens[s], scores, -jnp.inf)
        new0 = fresh[0, pl.ds(s, 1), :]
        new1 = fresh[1, pl.ds(s, 1), :]
        first = jnp.sum(q * new0, axis=1, keepdims=True) * SCALE
        second = jnp.sum(q * new1, axis=1, keepdims=True) * SCALE
        second = jnp.where(second_step, second, -jnp.inf)
        largest = jnp.maximum(jnp.max(scores, axis=1, keepdims=True), jnp.maximum(first, second))
        weights = jnp.exp(scores - largest)
        first = jnp.exp(first - largest)
        second = jnp.exp(second - largest)
        total = jnp.sum(weights, axis=1, keepdims=True) + first + second
        probs = (weights / total).astype(BF16)
        first = (first / total).astype(BF16).astype(F32)
        second = (second / total).astype(BF16).astype(F32)
        latent = dot_nt(probs, keys[0:LAT, :])
        latent = latent + first * new0[:, 0:LAT] + second * new1[:, 0:LAT]
        lat_send[:, pl.ds(s, 1)] = latent.reshape(16, 1, 8, LAT).astype(BF16)
        return carry

    lax.fori_loop(0, 4, attend, 0)

    moves = [
        exchange(lambda p: lat_send.at[p], lambda m: lat_recv.at[m], lat_s, lat_r, shift)
        for shift in range(1, groups)
    ]
    for move in moves:
        move.start()
    lat_recv[me] = lat_send[me]
    for move in moves:
        move.wait()

    rows = lat_recv[...].astype(F32).reshape(512, LAT).astype(BF16)
    row = lax.broadcasted_iota(jnp.int32, (128, 512), 0)
    col = lax.broadcasted_iota(jnp.int32, (128, 512), 1)
    base = (row >> 3) * 32 + (row & 3) * 8 + ((row >> 2) & 1) * 4
    heads = []
    for h in range(4):
        up = dot(rows, value_up[h]).astype(BF16)
        take = jnp.where(col == base + h, 1.0, 0.0).astype(BF16)
        heads.append(dot(take, up).astype(BF16))
    heads = jnp.concatenate(heads, axis=1)
    proj_copy.wait()

    def produce(p):
        start, width = PROJ_PARTS[p]
        chunk = 896
        for n in range(width // chunk):
            cols = pl.ds(start + n * chunk, chunk)
            part[:, :, :, cols] = dot(heads, proj[:, cols]).reshape(4, 4, 8, chunk).astype(BF16)

    def finish(p, cols, total):
        wide_sum[:, cols] = total

    ring_sum(
        at, PROJ_ORDERS, ((0, 1), (2, 3)), PROJ_PARTS, part, ((h0l, h0r), (h1l, h1r)),
        ((f0l, f0r), (f1l, f1r)), part_s, part_r, neighbour, produce, finish,
    )

    chunk = 1024
    square = jnp.zeros((8, 1), F32)
    for n in range(model // chunk):
        cols = pl.ds(n * chunk, chunk)
        total = wide_sum[:, cols] + jnp.concatenate(
            [resid[0, :, cols].astype(F32), resid[1, :, cols].astype(F32)], axis=0
        )
        stream = total.astype(BF16)
        stream_out[:, cols] = stream
        wide = stream.astype(F32)
        square = square + jnp.sum(wide * wide, axis=1, keepdims=True)
    scale = lax.rsqrt(square * (1.0 / model) + EPS)
    for n in range(model // chunk):
        cols = pl.ds(n * chunk, chunk)
        wide = stream_out[:, cols].astype(F32)
        normed_out[:, cols] = (wide * scale * gain[:, cols]).astype(BF16)


PARTS = ((0, 1280), (2432, 1280), (4864, 1280), (1280, 1152), (3712, 1152), (6144, 1152))
OUT_PARTS = PARTS[:5] + ((6144, 1024),)
STREAMS = ((0, 1, 2), (3, 4, 5))
ROW = 7296


def expert_kernel(
    normed, mix, stream, gate, up, down,
    out,
    rows, hid_w, down_w, acc, obuf,
    h0l, h0r, f0l, f0r, h1l, h1r, f1l, f1r, h2l, h2r, f2l, f2r,
    g_send, g_recv, s_send, s_recv, w_send, w_recv, w_local,
):
    dp = lax.axis_index("dp")
    tp = lax.axis_index("tp")
    at = (dp // 4, dp % 4, tp // 2)
    core = tp % 2
    signs = (1, -1)
    every = slice(None)

    def neighbour(axis, sign):
        new = list(at)
        new[axis] = (at[axis] + sign + 4) % 4
        return (new[0] * 4 + new[1], new[2] * 2 + core)

    partner = (dp, (tp // 2) * 2 + (1 - core))

    barrier = pltpu.get_barrier_semaphore()
    for axis in range(3):
        for sign in signs:
            pl.semaphore_signal(
                barrier, inc=1, device_id=neighbour(axis, sign), device_id_type=MESH
            )
    pl.semaphore_signal(barrier, inc=1, device_id=partner, device_id_type=MESH)

    rows[at[0], at[1], at[2], :, 0:7168] = normed[...]
    rows[at[0], at[1], at[2], :, 7168:7296] = mix[...]
    local = []
    remote = []

    def spots(e, which):
        if which < 2:
            base = e * 512 + which * 256
            return hid_w.at[:, pl.ds(base, 128)], hid_w.at[:, pl.ds(base + 128, 128)]
        return down_w.at[pl.ds(e * 256, 128)], down_w.at[pl.ds(e * 256 + 128, 128)]

    for e in range(2):
        for which, ref in enumerate((gate, up, down)):
            mine, theirs = spots(e, which)
            n = e * 3 + which
            local.append(pltpu.make_async_copy(ref.at[e], mine, w_local.at[n]))
            remote.append(
                pltpu.make_async_remote_copy(
                    src_ref=ref.at[e],
                    dst_ref=theirs,
                    send_sem=w_send.at[n],
                    recv_sem=w_recv.at[n],
                    device_id=partner,
                    device_id_type=MESH,
                )
            )
    for copy in local:
        copy.start()
    pl.semaphore_wait(barrier, 7)

    order = [(p % 3, (p + 1) % 3, (p + 2) % 3) for p in range(6)]

    def shifted(axis, offset):
        return (at[axis] + offset + 4) % 4

    def block(p, values, start, width):
        where = [None] * 3
        for axis, value in zip(order[p], values):
            where[axis] = every if value is None else value
        return tuple(where) + (every, pl.ds(start, width))

    def known(phase, p, offset):
        values = [None] * phase + [shifted(order[p][phase], offset)]
        return values + [at[axis] for axis in order[p][phase + 1:]]

    def push(phase, p, offset, k, step, columns):
        ref = rows.at[block(p, known(phase, p, offset), *columns)]
        slot = (phase * 6 + p) * 4 + step * 2 + k
        copy = pltpu.make_async_remote_copy(
            src_ref=ref,
            dst_ref=ref,
            send_sem=g_send.at[slot],
            recv_sem=g_recv.at[slot],
            device_id=neighbour(order[p][phase], signs[k]),
            device_id_type=MESH,
        )
        copy.start()
        return copy

    one, two = {}, {}

    def step_one(phase, p):
        if phase > 0:
            for k in range(2):
                two[phase - 1, p, k].wait_recv()
        for k in range(2):
            one[phase, p, k] = push(phase, p, 0, k, 0, PARTS[p])

    def step_two(phase, p):
        for k in range(2):
            one[phase, p, k].wait_recv()
            two[phase, p, k] = push(phase, p, -signs[k], k, 1, halves(*PARTS[p])[k])

    for phase in range(3):
        for group in STREAMS:
            for p in group:
                step_one(phase, p)
        if phase == 0:
            for copy in remote:
                copy.start()
            acc[...] = jnp.zeros_like(acc)
        if phase < 2:
            for group in STREAMS:
                for p in group:
                    step_two(phase, p)

    for copy in local:
        copy.wait()
    for copy in remote:
        copy.wait()

    def multiply(p, offset):
        start, width = OUT_PARTS[p]
        lhs = rows[block(p, known(2, p, offset), start, width)]
        lhs = lhs.astype(F32).reshape(128, width).astype(BF16)
        for n in range(4):
            cols = (n * 256, 256)
            where = block(p, known(2, p, offset), *cols)
            product = dot(lhs, hid_w[pl.ds(start, width), pl.ds(*cols)])
            acc[where] = acc[where] + product.reshape(4, 4, 8, 256)

    for p in range(6):
        multiply(p, 0)
    for group in STREAMS:
        for p in group:
            step_two(2, p)
    for p in range(6):
        multiply(p, 1)
        multiply(p, -1)
    for p in range(6):
        for k in range(2):
            two[2, p, k].wait_recv()
        multiply(p, 2)
    for copy in list(one.values()) + list(two.values()):
        copy.wait_send()

    lanes = lax.broadcasted_iota(jnp.int32, (512, 128), 1)
    table = rows[:, :, :, :, 7168:7296].astype(F32).reshape(512, 128)
    hidden = []
    for e in range(2):
        expert = dp * 2 + e
        mine = (lanes == expert) | (lanes == expert + 32)
        weight = jnp.sum(jnp.where(mine, table, 0.0), axis=1, keepdims=True)
        gate_act = acc[:, :, :, :, e * 512:e * 512 + 256].reshape(512, 256)
        up_act = acc[:, :, :, :, e * 512 + 256:e * 512 + 512].reshape(512, 256)
        hidden.append((gate_act / (1.0 + jnp.exp(-gate_act)) * up_act * weight).astype(BF16))
    hidden = jnp.concatenate(hidden, axis=1)

    def produce(p):
        start, width = OUT_PARTS[p]
        for done in range(0, width, 256):
            size = min(256, width - done)
            cols = pl.ds(start + done, size)
            obuf[:, :, :, :, cols] = (
                dot(hidden, down_w[:, cols]).reshape(4, 4, 4, 8, size).astype(BF16)
            )

    def finish(p, cols, total):
        total = total + stream[:, cols].astype(F32)
        out[0, :, cols] = total[0:4].astype(BF16)
        out[1, :, cols] = total[4:8].astype(BF16)

    ring_sum(
        at, [o[::-1] for o in order], STREAMS, OUT_PARTS, obuf, ((h0l, h0r), (h1l, h1r), (h2l, h2r)),
        ((f0l, f0r), (f1l, f1r), (f2l, f2r)), s_send, s_recv, neighbour, produce, finish,
    )


def per_device(
    cache_pool, send_plan, tables, lengths, new_latent, queries, value_up, out_proj, residual,
    norm_gain, routes, route_weight, gate_proj, up_proj, down_proj,
):
    model = residual.shape[2]
    vmem = pl.BlockSpec(memory_space=pltpu.VMEM)
    smem = pl.BlockSpec(memory_space=pltpu.SMEM)
    hbm = pl.BlockSpec(memory_space=pl.ANY)
    dma = pltpu.SemaphoreType.DMA


    def rings(parts, shape, width):
        return [pltpu.VMEM((parts,) + shape + (8, width), BF16)] * 2

    scratch = [
        pltpu.VMEM((2, 4, 4, 576, 128), BF16),
        pltpu.VMEM((2, 4, 4, 576, 128), BF16),
        pltpu.VMEM((2, 2, 2, 576, 128), BF16),
        pltpu.VMEM((2, 2, 2, 576, 128), BF16),
        pltpu.VMEM((2, 4, 4, 576, 128), BF16),
        pltpu.VMEM((576, 1024), BF16),
        pltpu.VMEM((2, 4, 576), F32),
        pltpu.VMEM((16, 4, 8, LAT), BF16),
        pltpu.VMEM((16, 4, 8, LAT), BF16),
        pltpu.VMEM((512, model), BF16),
        pltpu.VMEM((4, 4, 8, model), BF16),
        pltpu.VMEM((8, model), F32),
    ]
    for shape in ((4,), ()):
        scratch += rings(4, shape, 896)
        scratch += rings(4, shape, 1792)
    scratch += [dma((24,)), dma((24,)), dma((15,)), dma((15,)), dma((32,)), dma((32,)), dma((5,))]
    stream, normed = pl.pallas_call(
        attention_kernel,
        out_shape=(
            jax.ShapeDtypeStruct((8, model), BF16),
            jax.ShapeDtypeStruct((8, model), BF16),
        ),
        in_specs=[smem, smem, smem, vmem, vmem, vmem, vmem, hbm, vmem, vmem],
        out_specs=(vmem, vmem),
        scratch_shapes=scratch,
        compiler_params=pltpu.CompilerParams(
            collective_id=0, has_side_effects=True, vmem_limit_bytes=56 * MIB
        ),
        name="attention",
    )(
        jnp.transpose(send_plan, (0, 2, 1)), tables, lengths, cache_pool, queries, new_latent, value_up,
        out_proj, residual, norm_gain.reshape(1, model),
    )

    matches = routes.reshape(8, 8)[:, :, None] == jnp.arange(32, dtype=jnp.int32)[None, None, :]
    dense = jnp.sum(jnp.where(matches, route_weight.reshape(8, 8)[:, :, None], 0.0), axis=1)
    high = lax.reduce_precision(dense, 8, 7)
    mix = jnp.concatenate([high, dense - high, jnp.zeros((8, 64), F32)], axis=1).astype(BF16)

    scratch = [
        pltpu.VMEM((4, 4, 4, 8, ROW), BF16),
        pltpu.VMEM((model, 1024), BF16),
        pltpu.VMEM((512, model), BF16),
        pltpu.VMEM((4, 4, 4, 8, 1024), F32),
        pltpu.VMEM((4, 4, 4, 8, model), BF16),
    ]
    for shape in ((4, 4), (4,), ()):
        scratch += rings(6, shape, 640)
        scratch += rings(6, shape, 1280)
    scratch += [dma((n,)) for n in (72, 72, 72, 72, 6, 6, 6)]
    result = pl.pallas_call(
        expert_kernel,
        out_shape=jax.ShapeDtypeStruct(residual.shape, BF16),
        in_specs=[vmem, vmem, vmem, hbm, hbm, hbm],
        out_specs=vmem,
        scratch_shapes=scratch,
        compiler_params=pltpu.CompilerParams(
            collective_id=1, has_side_effects=True, vmem_limit_bytes=60 * MIB
        ),
        name="experts",
    )(normed, mix, stream, gate_proj, up_proj, down_proj)
    return result


def solution(mesh):
    placed = (
        P(("dp", "tp"), None, None),
        P(("dp", "tp"), None, None),
        P(("dp", "tp"), None),
        P(("dp", "tp")),
        P(None, ("dp", "tp"), None),
        P(None, ("dp", "tp"), None, None),
        P("dp", None, None),
        P("dp", None),
        P(None, ("dp", "tp"), None),
        P(),
        P(None, ("dp", "tp"), None),
        P(None, ("dp", "tp"), None),
        P("dp", None, "tp"),
        P("dp", None, "tp"),
        P("dp", "tp", None),
    )
    return jax.shard_map(
        per_device,
        mesh=mesh,
        in_specs=placed,
        out_specs=P(None, ("dp", "tp"), None),
        check_vma=False,
    )
```

```python
import functools

import jax
import jax.numpy as jnp
from jax import lax
from jax.experimental import pallas as pl
from jax.experimental.pallas import tpu as pltpu
from jax.sharding import PartitionSpec as P

MESH = pl.DeviceIdType.MESH
F32 = jnp.float32
BF16 = jnp.bfloat16
LAT = 512
SCALE = 1.0 / 13.856406460551018
EPS = 1e-06
MIB = 1 << 20


def dot(a, b):
    return jnp.dot(a, b, preferred_element_type=F32)


def dot_nt(a, b):
    return lax.dot_general(a, b, (((1,), (1,)), ((), ())), preferred_element_type=F32)


def halves(start, width):
    tiles = width // 128
    first = (tiles + 1) // 2 * 128
    return (start, first), (start + first, width - first)


def ring_sum(
    at, orders, streams, parts, buf, half_in, full_in, last_in, sends, recvs, neighbour, produce, finish
):
    axes = len(orders[0])
    count = len(parts)
    signs = (1, -1)
    far, near = {}, {}

    def place(phase, p, offset):
        where = [slice(None)] * axes
        for a in orders[p][:phase]:
            where[a] = at[a]
        axis = orders[p][phase]
        where[axis] = (at[axis] + offset + 4) % 4
        return tuple(where) + (slice(None),)

    def landing(refs, phase, p, k, width):
        return refs[phase][k].at[(p,) + (slice(None),) * (axes - phase) + (pl.ds(0, width),)]

    def push(src, dst, slot, axis, sign):
        copy = pltpu.make_async_remote_copy(
            src_ref=src,
            dst_ref=dst,
            send_sem=sends.at[slot],
            recv_sem=recvs.at[slot],
            device_id=neighbour(axis, sign),
            device_id_type=MESH,
        )
        copy.start()
        return copy

    def send_far(phase, p):
        for k in range(2):
            start, width = halves(*parts[p])[k]
            far[phase, p, k] = push(
                buf.at[place(phase, p, 2) + (pl.ds(start, width),)],
                landing(half_in, phase, p, k, width),
                (phase * count + p) * 4 + k, orders[p][phase], signs[k],
            )

    def send_near(phase, p, k):
        far[phase, p, k].wait_recv()
        start, width = halves(*parts[p])[k]
        half = place(phase, p, signs[k]) + (pl.ds(start, width),)
        buf[half] = (
            buf[half].astype(F32) + landing(half_in, phase, p, k, width)[...].astype(F32)
        ).astype(BF16)
        near[phase, p, k] = push(
            buf.at[place(phase, p, signs[k]) + (pl.ds(*parts[p]),)],
            landing(full_in, phase, p, k, parts[p][1]),
            (phase * count + p) * 4 + 2 + k, orders[p][phase], signs[k],
        )

    def send_last(p):
        phase = axes - 1
        for offset in (2, 1, 3):
            far[phase, p, offset] = push(
                buf.at[place(phase, p, offset) + (pl.ds(*parts[p]),)],
                last_in.at[p, offset - 1, :, pl.ds(0, parts[p][1])],
                (phase * count + p) * 4 + offset - 1, orders[p][phase], offset,
            )

    def last_sum(p):
        phase = axes - 1
        total = buf[place(phase, p, 0) + (pl.ds(*parts[p]),)].astype(F32)
        for offset in (1, 3, 2):
            far[phase, p, offset].wait_recv()
            total = total + last_in[p, offset - 1, :, pl.ds(0, parts[p][1])].astype(F32)
        return total

    def own_sum(phase, p):
        where = place(phase, p, 0) + (pl.ds(*parts[p]),)
        total = buf[where].astype(F32)
        for k in range(2):
            near[phase, p, k].wait_recv()
            total = total + landing(full_in, phase, p, k, parts[p][1])[...].astype(F32)
        buf[where] = total.astype(BF16)

    for phase in range(axes - 1):
        for stream in streams:
            for p in stream:
                if phase == 0:
                    produce(p)
                else:
                    own_sum(phase - 1, p)
                send_far(phase, p)
        for stream in streams:
            for p in stream:
                for k in range(2):
                    send_near(phase, p, k)
    for stream in streams:
        for p in stream:
            own_sum(axes - 2, p)
            send_last(p)
    for stream in streams:
        for p in stream:
            finish(p, pl.ds(*parts[p]), last_sum(p))
    for copy in list(far.values()) + list(near.values()):
        copy.wait_send()


PROJ_PARTS = ((0, 1792), (3584, 1792), (1792, 1792), (5376, 1792))
PROJ_ORDERS = ((1, 0), (0, 1), (1, 0), (0, 1))


def attention_kernel(
    plan, tab, lens, pool, queries, new_latent, value_up, proj_hbm, resid, gain, routes, route_weight,
    stream_out, normed_out, mix_out,
    outgoing, middle, near_fwd, far_fwd, arrived, keys, fresh, lat_send, lat_recv, proj, part,
    wide_sum, h0l, h0r, f0l, f0r, last,
    mig_s, mig_r, lat_s, lat_r, part_s, part_r, local_sem,
):
    groups = 16
    me = lax.axis_index("dp")
    lane = lax.axis_index("tp")
    at = (me // 4, me % 4)
    model = proj_hbm.shape[1]

    proj_copy = pltpu.make_async_copy(proj_hbm, proj, local_sem.at[0])
    proj_copy.start()

    def neighbour(axis, sign):
        new = list(at)
        new[axis] = (at[axis] + sign + 4) % 4
        return (new[0] * 4 + new[1], lane)

    barrier = pltpu.get_barrier_semaphore()
    for shift in range(1, groups):
        pl.semaphore_signal(
            barrier, inc=1, device_id=(lax.rem(me + shift, groups), lane), device_id_type=MESH
        )

    for c in range(2):
        def pick(i, carry):
            outgoing[c, i // 4, i % 4] = pool[jnp.maximum(plan[0, c, i], 0)]
            return carry

        lax.fori_loop(0, groups, pick, 0)
    for k in range(2):
        fresh[k] = new_latent[k].astype(F32)

    named = jnp.concatenate([routes[0], routes[1]], axis=0)
    given = jnp.concatenate([route_weight[0], route_weight[1]], axis=0)
    lanes = lax.broadcasted_iota(jnp.int32, (8, 128), 1)
    dense = jnp.zeros((8, 128), F32)
    for k in range(8):
        hit = ((lanes & 31) == named[:, k:k + 1]) & (lanes < 64)
        dense = dense + jnp.where(hit, given[:, k:k + 1], 0.0)
    high = dense.astype(BF16).astype(F32)
    mix_out[...] = jnp.where(lanes < 32, high, dense - high).astype(BF16)
    pl.semaphore_wait(barrier, groups - 1)

    def push(src, dst, slot, axis, sign):
        copy = pltpu.make_async_remote_copy(
            src_ref=src,
            dst_ref=dst,
            send_sem=mig_s.at[slot],
            recv_sem=mig_r.at[slot],
            device_id=neighbour(axis, sign),
            device_id_type=MESH,
        )
        copy.start()
        return copy

    def pair_at(axis, value, k):
        rest = pl.ds(0, 4) if k is None else pl.ds(2 * k, 2)
        return (rest, value) if axis == 1 else (value, rest)

    def local(src, dst, n):
        copy = pltpu.make_async_copy(src, dst, local_sem.at[n])
        copy.start()
        return copy

    for stage in range(2):
        source, target = (outgoing, middle) if stage == 0 else (middle, arrived)
        fwd = (near_fwd, far_fwd)[stage]
        first, kept = [], []
        for c in range(2):
            axis = 1 - c if stage == 0 else c
            far = (at[axis] + 2) % 4
            for k, sign in enumerate((1, -1)):
                base = ((stage * 2 + c) * 2 + k) * 3
                halfway = push(
                    source.at[(c,) + pair_at(axis, far, k)], fwd.at[c, k], base, axis, sign
                )
                beside = push(
                    source.at[(c,) + pair_at(axis, (at[axis] + sign + 4) % 4, None)],
                    target.at[(c,) + pair_at(axis, at[axis], None)],
                    base + 1, axis, sign,
                )
                first.append((c, k, sign, axis, base, halfway, beside))
            own = (c,) + pair_at(axis, at[axis], None)
            kept.append(local(source.at[own], target.at[own], 1 + stage * 2 + c))
        second = []
        for c, k, sign, axis, base, halfway, beside in first:
            halfway.wait_recv()
            came = (at[axis] - sign + 4) % 4
            second.append(
                push(fwd.at[c, k], target.at[(c,) + pair_at(axis, came, k)], base + 2, axis, sign)
            )
        for c, k, sign, axis, base, halfway, beside in first:
            halfway.wait_send()
            beside.wait()
        for copy in second + kept:
            copy.wait()

    row = lax.broadcasted_iota(jnp.int32, (128, 128), 0)
    col = lax.broadcasted_iota(jnp.int32, (128, 128), 1)
    reorder = jnp.where(
        col == ((row >> 2) & 1) * 64 + (row >> 3) * 4 + (row & 3), 1.0, 0.0
    ).astype(BF16)
    second_step = ((lax.broadcasted_iota(jnp.int32, (128, 1), 0) >> 2) & 1) == 1
    position = lax.broadcasted_iota(jnp.int32, (128, 1024), 1)

    def attend(s, carry):
        for j in range(8):
            entry = tab[s, j]
            own = pool[jnp.minimum(entry, 23)]
            came = jnp.maximum(entry - 24, 0)
            moved = arrived[came & 1, came >> 3, (came >> 1) & 3]
            keys[:, j * 128:(j + 1) * 128] = jnp.where(entry < 24, own, moved)
        q = jnp.concatenate([queries[0, s], queries[1, s]], axis=0)
        q = dot(reorder, q)
        q16 = q.astype(BF16)
        scores = dot(q16, keys[...]) * SCALE
        scores = jnp.where(position < lens[s], scores, -jnp.inf)
        new0 = fresh[0, pl.ds(s, 1), :]
        new1 = fresh[1, pl.ds(s, 1), :]
        first = jnp.sum(q * new0, axis=1, keepdims=True) * SCALE
        second = jnp.sum(q * new1, axis=1, keepdims=True) * SCALE
        second = jnp.where(second_step, second, -jnp.inf)
        largest = jnp.maximum(jnp.max(scores, axis=1, keepdims=True), jnp.maximum(first, second))
        weights = jnp.exp(scores - largest)
        first = jnp.exp(first - largest)
        second = jnp.exp(second - largest)
        total = jnp.sum(weights, axis=1, keepdims=True) + first + second
        probs = (weights / total).astype(BF16)
        first = (first / total).astype(BF16).astype(F32)
        second = (second / total).astype(BF16).astype(F32)
        latent = dot_nt(probs, keys[0:LAT, :])
        latent = latent + first * new0[:, 0:LAT] + second * new1[:, 0:LAT]
        lat_send[:, pl.ds(s, 1)] = latent.reshape(16, 1, 8, LAT).astype(BF16)
        return carry

    moves = []
    for half in range(2):
        lax.fori_loop(2 * half, 2 * half + 2, attend, 0)
        pair = pl.ds(2 * half, 2)
        for shift in range(1, groups):
            peer = lax.rem(me + shift, groups)
            slot = half * (groups - 1) + shift - 1
            move = pltpu.make_async_remote_copy(
                src_ref=lat_send.at[peer, pair],
                dst_ref=lat_recv.at[me, pair],
                send_sem=lat_s.at[slot],
                recv_sem=lat_r.at[slot],
                device_id=(peer, lane),
                device_id_type=MESH,
            )
            move.start()
            moves.append(move)
    lat_recv[me] = lat_send[me]
    for move in moves:
        move.wait()

    rows = lat_recv[...].astype(F32).reshape(512, LAT).astype(BF16)
    row = lax.broadcasted_iota(jnp.int32, (128, 512), 0)
    col = lax.broadcasted_iota(jnp.int32, (128, 512), 1)
    base = (row >> 3) * 32 + (row & 3) * 8 + ((row >> 2) & 1) * 4
    heads = []
    for h in range(4):
        up = dot(rows, value_up[h]).astype(BF16)
        take = jnp.where(col == base + h, 1.0, 0.0).astype(BF16)
        heads.append(dot(take, up).astype(BF16))
    heads = jnp.concatenate(heads, axis=1)
    proj_copy.wait()

    def produce(p):
        start, width = PROJ_PARTS[p]
        chunk = 896
        for n in range(width // chunk):
            cols = pl.ds(start + n * chunk, chunk)
            part[:, :, :, cols] = dot(heads, proj[:, cols]).reshape(4, 4, 8, chunk).astype(BF16)

    def finish(p, cols, total):
        wide_sum[:, cols] = total

    ring_sum(
        at, PROJ_ORDERS, ((0, 1), (2, 3)), PROJ_PARTS, part, ((h0l, h0r),),
        ((f0l, f0r),), last, part_s, part_r, neighbour, produce, finish,
    )

    chunk = 1024
    square = jnp.zeros((8, 1), F32)
    for n in range(model // chunk):
        cols = pl.ds(n * chunk, chunk)
        total = wide_sum[:, cols] + jnp.concatenate(
            [resid[0, :, cols].astype(F32), resid[1, :, cols].astype(F32)], axis=0
        )
        stream = total.astype(BF16)
        stream_out[:, cols] = stream
        wide = stream.astype(F32)
        square = square + jnp.sum(wide * wide, axis=1, keepdims=True)
    scale = lax.rsqrt(square * (1.0 / model) + EPS)
    for n in range(model // chunk):
        cols = pl.ds(n * chunk, chunk)
        wide = stream_out[:, cols].astype(F32)
        normed_out[:, cols] = (wide * scale * gain[:, cols]).astype(BF16)


PARTS = ((0, 1280), (2432, 1280), (4864, 1280), (1280, 1152), (3712, 1152), (6144, 1152))
OUT_PARTS = PARTS[:5] + ((6144, 1024),)
STREAMS = ((0, 1, 2), (3, 4, 5))
ROW = 7296


def expert_kernel(
    normed, mix, stream, gate, up, down,
    out,
    rows, hid_w, down_w, acc, obuf,
    h0l, h0r, f0l, f0r, h1l, h1r, f1l, f1r, last,
    g_send, g_recv, s_send, s_recv, w_send, w_recv, w_local,
):
    dp = lax.axis_index("dp")
    tp = lax.axis_index("tp")
    at = (dp // 4, dp % 4, tp // 2)
    core = tp % 2
    signs = (1, -1)
    every = slice(None)

    def neighbour(axis, sign):
        new = list(at)
        new[axis] = (at[axis] + sign + 4) % 4
        return (new[0] * 4 + new[1], new[2] * 2 + core)

    partner = (dp, (tp // 2) * 2 + (1 - core))

    barrier = pltpu.get_barrier_semaphore()
    for axis in range(3):
        for sign in (1, 2, 3):
            pl.semaphore_signal(
                barrier, inc=1, device_id=neighbour(axis, sign), device_id_type=MESH
            )
    pl.semaphore_signal(barrier, inc=1, device_id=partner, device_id_type=MESH)

    rows[at[0], at[1], at[2], :, 0:7168] = normed[...]
    rows[at[0], at[1], at[2], :, 7168:7296] = mix[...]
    local = []
    remote = []

    def spots(e, which):
        if which < 2:
            base = e * 512 + which * 256
            return hid_w.at[:, pl.ds(base, 128)], hid_w.at[:, pl.ds(base + 128, 128)]
        return down_w.at[pl.ds(e * 256, 128)], down_w.at[pl.ds(e * 256 + 128, 128)]

    for e in range(2):
        for which, ref in enumerate((gate, up, down)):
            mine, theirs = spots(e, which)
            n = e * 3 + which
            local.append(pltpu.make_async_copy(ref.at[e], mine, w_local.at[n]))
            remote.append(
                pltpu.make_async_remote_copy(
                    src_ref=ref.at[e],
                    dst_ref=theirs,
                    send_sem=w_send.at[n],
                    recv_sem=w_recv.at[n],
                    device_id=partner,
                    device_id_type=MESH,
                )
            )
    for copy in local:
        copy.start()
    pl.semaphore_wait(barrier, 10)

    order = [(p % 3, (p + 1) % 3, (p + 2) % 3) for p in range(6)]

    def shifted(axis, offset):
        return (at[axis] + offset + 4) % 4

    def block(p, values, start, width):
        where = [None] * 3
        for axis, value in zip(order[p], values):
            where[axis] = every if value is None else value
        return tuple(where) + (every, pl.ds(start, width))

    def known(phase, p, offset):
        values = [None] * phase + [shifted(order[p][phase], offset)]
        return values + [at[axis] for axis in order[p][phase + 1:]]

    def push(phase, p, offset, slot, sign, columns):
        ref = rows.at[block(p, known(phase, p, offset), *columns)]
        slot = (phase * 6 + p) * 4 + slot
        copy = pltpu.make_async_remote_copy(
            src_ref=ref,
            dst_ref=ref,
            send_sem=g_send.at[slot],
            recv_sem=g_recv.at[slot],
            device_id=neighbour(order[p][phase], sign),
            device_id_type=MESH,
        )
        copy.start()
        return copy

    one, two = {}, {}

    def step_one(phase, p):
        if phase == 0:
            for sign in (2, 1, 3):
                two[0, p, sign - 1] = push(0, p, 0, sign - 1, sign, PARTS[p])
            return
        for k in range(3 if phase == 1 else 2):
            two[phase - 1, p, k].wait_recv()
        for k in range(2):
            one[phase, p, k] = push(phase, p, 0, k, signs[k], PARTS[p])

    def step_two(phase, p):
        for k in range(2):
            one[phase, p, k].wait_recv()
            two[phase, p, k] = push(phase, p, -signs[k], 2 + k, signs[k], halves(*PARTS[p])[k])

    for phase in range(3):
        for group in STREAMS:
            for p in group:
                step_one(phase, p)
        if phase == 0:
            for copy in remote:
                copy.start()
            acc[...] = jnp.zeros_like(acc)
        if phase == 1:
            for group in STREAMS:
                for p in group:
                    step_two(phase, p)

    for copy in local:
        copy.wait()
    for copy in remote:
        copy.wait()

    def multiply(p, offset):
        start, width = OUT_PARTS[p]
        lhs = rows[block(p, known(2, p, offset), start, width)]
        lhs = lhs.astype(F32).reshape(128, width).astype(BF16)
        for n in range(4):
            cols = (n * 256, 256)
            where = block(p, known(2, p, offset), *cols)
            product = dot(lhs, hid_w[pl.ds(start, width), pl.ds(*cols)])
            acc[where] = acc[where] + product.reshape(4, 4, 8, 256)

    for p in range(6):
        multiply(p, 0)
    for group in STREAMS:
        for p in group:
            step_two(2, p)
    for p in range(6):
        multiply(p, 1)
        multiply(p, -1)
    for p in range(6):
        for k in range(2):
            two[2, p, k].wait_recv()
        multiply(p, 2)
    for copy in list(one.values()) + list(two.values()):
        copy.wait_send()

    lanes = lax.broadcasted_iota(jnp.int32, (512, 128), 1)
    table = rows[:, :, :, :, 7168:7296].astype(F32).reshape(512, 128)
    hidden = []
    for e in range(2):
        expert = dp * 2 + e
        mine = (lanes == expert) | (lanes == expert + 32)
        weight = jnp.sum(jnp.where(mine, table, 0.0), axis=1, keepdims=True)
        gate_act = acc[:, :, :, :, e * 512:e * 512 + 256].reshape(512, 256)
        up_act = acc[:, :, :, :, e * 512 + 256:e * 512 + 512].reshape(512, 256)
        hidden.append((gate_act / (1.0 + jnp.exp(-gate_act)) * up_act * weight).astype(BF16))
    hidden = jnp.concatenate(hidden, axis=1)

    def produce(p):
        start, width = OUT_PARTS[p]
        for done in range(0, width, 256):
            size = min(256, width - done)
            cols = pl.ds(start + done, size)
            obuf[:, :, :, :, cols] = (
                dot(hidden, down_w[:, cols]).reshape(4, 4, 4, 8, size).astype(BF16)
            )

    def finish(p, cols, total):
        total = total + stream[:, cols].astype(F32)
        out[0, :, cols] = total[0:4].astype(BF16)
        out[1, :, cols] = total[4:8].astype(BF16)

    ring_sum(
        at, [o[::-1] for o in order], STREAMS, OUT_PARTS, obuf, ((h0l, h0r), (h1l, h1r)),
        ((f0l, f0r), (f1l, f1r)), last, s_send, s_recv, neighbour, produce, finish,
    )


def per_device(
    cache_pool, send_plan, tables, lengths, new_latent, queries, value_up, out_proj, residual,
    norm_gain, routes, route_weight, gate_proj, up_proj, down_proj,
):
    model = residual.shape[2]
    vmem = pl.BlockSpec(memory_space=pltpu.VMEM)
    smem = pl.BlockSpec(memory_space=pltpu.SMEM)
    hbm = pl.BlockSpec(memory_space=pl.ANY)
    dma = pltpu.SemaphoreType.DMA


    def rings(parts, shape, width):
        return [pltpu.VMEM((parts,) + shape + (8, width), BF16)] * 2

    scratch = [
        pltpu.VMEM((2, 4, 4, 576, 128), BF16),
        pltpu.VMEM((2, 4, 4, 576, 128), BF16),
        pltpu.VMEM((2, 2, 2, 576, 128), BF16),
        pltpu.VMEM((2, 2, 2, 576, 128), BF16),
        pltpu.VMEM((2, 4, 4, 576, 128), BF16),
        pltpu.VMEM((576, 1024), BF16),
        pltpu.VMEM((2, 4, 576), F32),
        pltpu.VMEM((16, 4, 8, LAT), BF16),
        pltpu.VMEM((16, 4, 8, LAT), BF16),
        pltpu.VMEM((512, model), BF16),
        pltpu.VMEM((4, 4, 8, model), BF16),
        pltpu.VMEM((8, model), F32),
    ]
    scratch += rings(4, (4,), 896)
    scratch += rings(4, (4,), 1792)
    scratch.append(pltpu.VMEM((4, 3, 8, 1792), BF16))
    scratch += [dma((24,)), dma((24,)), dma((30,)), dma((30,)), dma((32,)), dma((32,)), dma((5,))]
    stream, normed, mix = pl.pallas_call(
        attention_kernel,
        out_shape=(
            jax.ShapeDtypeStruct((8, model), BF16),
            jax.ShapeDtypeStruct((8, model), BF16),
            jax.ShapeDtypeStruct((8, 128), BF16),
        ),
        in_specs=[smem, smem, smem, vmem, vmem, vmem, vmem, hbm, vmem, vmem, vmem, vmem],
        out_specs=(vmem, vmem, vmem),
        scratch_shapes=scratch,
        compiler_params=pltpu.CompilerParams(
            collective_id=0, has_side_effects=True, vmem_limit_bytes=56 * MIB
        ),
        name="attention",
    )(
        jnp.transpose(send_plan, (0, 2, 1)), tables, lengths, cache_pool, queries, new_latent, value_up,
        out_proj, residual, norm_gain.reshape(1, model), routes, route_weight,
    )

    scratch = [
        pltpu.VMEM((4, 4, 4, 8, ROW), BF16),
        pltpu.VMEM((model, 1024), BF16),
        pltpu.VMEM((512, model), BF16),
        pltpu.VMEM((4, 4, 4, 8, 1024), F32),
        pltpu.VMEM((4, 4, 4, 8, model), BF16),
    ]
    for shape in ((4, 4), (4,)):
        scratch += rings(6, shape, 640)
        scratch += rings(6, shape, 1280)
    scratch.append(pltpu.VMEM((6, 3, 8, 1280), BF16))
    scratch += [dma((n,)) for n in (72, 72, 72, 72, 6, 6, 6)]
    result = pl.pallas_call(
        expert_kernel,
        out_shape=jax.ShapeDtypeStruct(residual.shape, BF16),
        in_specs=[vmem, vmem, vmem, hbm, hbm, hbm],
        out_specs=vmem,
        scratch_shapes=scratch,
        compiler_params=pltpu.CompilerParams(
            collective_id=1, has_side_effects=True, vmem_limit_bytes=60 * MIB
        ),
        name="experts",
    )(normed, mix, stream, gate_proj, up_proj, down_proj)
    return result


def solution(mesh):
    placed = (
        P(("dp", "tp"), None, None),
        P(("dp", "tp"), None, None),
        P(("dp", "tp"), None),
        P(("dp", "tp")),
        P(None, ("dp", "tp"), None),
        P(None, ("dp", "tp"), None, None),
        P("dp", None, None),
        P("dp", None),
        P(None, ("dp", "tp"), None),
        P(),
        P(None, ("dp", "tp"), None),
        P(None, ("dp", "tp"), None),
        P("dp", None, "tp"),
        P("dp", None, "tp"),
        P("dp", "tp", None),
    )
    return jax.shard_map(
        per_device,
        mesh=mesh,
        in_specs=placed,
        out_specs=P(None, ("dp", "tp"), None),
        check_vma=False,
    )
```

```python
import functools

import jax
import jax.numpy as jnp
from jax import lax
from jax.experimental import pallas as pl
from jax.experimental.pallas import tpu as pltpu
from jax.sharding import PartitionSpec as P

MESH = pl.DeviceIdType.MESH
F32 = jnp.float32
BF16 = jnp.bfloat16
LAT = 512
SCALE = 1.0 / 13.856406460551018
EPS = 1e-06
MIB = 1 << 20


def dot(a, b):
    return jnp.dot(a, b, preferred_element_type=F32)


def dot_nt(a, b):
    return lax.dot_general(a, b, (((1,), (1,)), ((), ())), preferred_element_type=F32)


def halves(start, width):
    tiles = width // 128
    first = (tiles + 1) // 2 * 128
    return (start, first), (start + first, width - first)


def ring_sum(
    at, orders, streams, parts, buf, half_in, full_in, last_in, sends, recvs, neighbour, produce, finish
):
    axes = len(orders[0])
    count = len(parts)
    signs = (1, -1)
    far, near = {}, {}

    def place(phase, p, offset):
        where = [slice(None)] * axes
        for a in orders[p][:phase]:
            where[a] = at[a]
        axis = orders[p][phase]
        where[axis] = (at[axis] + offset + 4) % 4
        return tuple(where) + (slice(None),)

    def landing(refs, phase, p, k, width):
        return refs[phase][k].at[(p,) + (slice(None),) * (axes - phase) + (pl.ds(0, width),)]

    def push(src, dst, slot, axis, sign):
        copy = pltpu.make_async_remote_copy(
            src_ref=src,
            dst_ref=dst,
            send_sem=sends.at[slot],
            recv_sem=recvs.at[slot],
            device_id=neighbour(axis, sign),
            device_id_type=MESH,
        )
        copy.start()
        return copy

    def send_far(phase, p):
        for k in range(2):
            start, width = halves(*parts[p])[k]
            far[phase, p, k] = push(
                buf.at[place(phase, p, 2) + (pl.ds(start, width),)],
                landing(half_in, phase, p, k, width),
                (phase * count + p) * 4 + k, orders[p][phase], signs[k],
            )

    def send_near(phase, p, k):
        far[phase, p, k].wait_recv()
        start, width = halves(*parts[p])[k]
        half = place(phase, p, signs[k]) + (pl.ds(start, width),)
        buf[half] = (
            buf[half].astype(F32) + landing(half_in, phase, p, k, width)[...].astype(F32)
        ).astype(BF16)
        near[phase, p, k] = push(
            buf.at[place(phase, p, signs[k]) + (pl.ds(*parts[p]),)],
            landing(full_in, phase, p, k, parts[p][1]),
            (phase * count + p) * 4 + 2 + k, orders[p][phase], signs[k],
        )

    def send_last(p):
        phase = axes - 1
        for offset in (2, 1, 3):
            far[phase, p, offset] = push(
                buf.at[place(phase, p, offset) + (pl.ds(*parts[p]),)],
                last_in.at[p, offset - 1, :, pl.ds(0, parts[p][1])],
                (phase * count + p) * 4 + offset - 1, orders[p][phase], offset,
            )

    def last_sum(p):
        phase = axes - 1
        total = buf[place(phase, p, 0) + (pl.ds(*parts[p]),)].astype(F32)
        for offset in (1, 3, 2):
            far[phase, p, offset].wait_recv()
            total = total + last_in[p, offset - 1, :, pl.ds(0, parts[p][1])].astype(F32)
        return total

    def own_sum(phase, p):
        where = place(phase, p, 0) + (pl.ds(*parts[p]),)
        total = buf[where].astype(F32)
        for k in range(2):
            near[phase, p, k].wait_recv()
            total = total + landing(full_in, phase, p, k, parts[p][1])[...].astype(F32)
        buf[where] = total.astype(BF16)

    for phase in range(axes - 1):
        for stream in streams:
            for p in stream:
                if phase == 0:
                    produce(p)
                else:
                    own_sum(phase - 1, p)
                send_far(phase, p)
        for stream in streams:
            for p in stream:
                for k in range(2):
                    send_near(phase, p, k)
    for stream in streams:
        for p in stream:
            own_sum(axes - 2, p)
            send_last(p)
    for stream in streams:
        for p in stream:
            finish(p, pl.ds(*parts[p]), last_sum(p))
    for copy in list(far.values()) + list(near.values()):
        copy.wait_send()


PROJ_PARTS = ((0, 1792), (3584, 1792), (1792, 1792), (5376, 1792))
PROJ_ORDERS = ((1, 0), (0, 1), (1, 0), (0, 1))


def attention_kernel(
    plan, tab, lens, pool, queries, new_latent, value_up, proj_hbm, resid, gain, routes, route_weight,
    stream_out, normed_out, mix_out,
    outgoing, middle, near_fwd, far_fwd, arrived, keys, fresh, lat_send, lat_recv, proj, part,
    wide_sum, h0l, h0r, f0l, f0r, last,
    mig_s, mig_r, lat_s, lat_r, part_s, part_r, local_sem,
):
    groups = 16
    me = lax.axis_index("dp")
    lane = lax.axis_index("tp")
    at = (me // 4, me % 4)
    model = proj_hbm.shape[1]

    proj_copy = pltpu.make_async_copy(proj_hbm, proj, local_sem.at[0])
    proj_copy.start()

    def neighbour(axis, sign):
        new = list(at)
        new[axis] = (at[axis] + sign + 4) % 4
        return (new[0] * 4 + new[1], lane)

    barrier = pltpu.get_barrier_semaphore()
    for shift in range(1, groups):
        pl.semaphore_signal(
            barrier, inc=1, device_id=(lax.rem(me + shift, groups), lane), device_id_type=MESH
        )

    for c in range(2):
        def pick(i, carry):
            outgoing[c, i // 4, i % 4] = pool[jnp.maximum(plan[0, c, i], 0)]
            return carry

        lax.fori_loop(0, groups, pick, 0)
    for k in range(2):
        fresh[k] = new_latent[k].astype(F32)

    named = jnp.concatenate([routes[0], routes[1]], axis=0)
    given = jnp.concatenate([route_weight[0], route_weight[1]], axis=0)
    lanes = lax.broadcasted_iota(jnp.int32, (8, 128), 1)
    dense = jnp.zeros((8, 128), F32)
    for k in range(8):
        hit = ((lanes & 31) == named[:, k:k + 1]) & (lanes < 64)
        dense = dense + jnp.where(hit, given[:, k:k + 1], 0.0)
    high = dense.astype(BF16).astype(F32)
    mix_out[...] = jnp.where(lanes < 32, high, dense - high).astype(BF16)
    pl.semaphore_wait(barrier, groups - 1)

    def push(src, dst, slot, axis, sign):
        copy = pltpu.make_async_remote_copy(
            src_ref=src,
            dst_ref=dst,
            send_sem=mig_s.at[slot],
            recv_sem=mig_r.at[slot],
            device_id=neighbour(axis, sign),
            device_id_type=MESH,
        )
        copy.start()
        return copy

    def pair_at(c, axis, value, k, h):
        rest = pl.ds(0, 4) if k is None else pl.ds(2 * k, 2)
        where = (rest, value) if axis == 1 else (value, rest)
        return (c,) + where + (pl.ds(288 * h, 288),)

    def local(src, dst, n):
        copy = pltpu.make_async_copy(src, dst, local_sem.at[n])
        copy.start()
        return copy

    started, passed, kept = {}, {}, {}

    def send_bundles(stage, h):
        source, target = (outgoing, middle) if stage == 0 else (middle, arrived)
        fwd = (near_fwd, far_fwd)[stage]
        for c in range(2):
            axis = 1 - c if stage == 0 else c
            far = (at[axis] + 2) % 4
            for k, sign in enumerate((1, -1)):
                base = (((stage * 2 + h) * 2 + c) * 2 + k) * 3
                halfway = push(
                    source.at[pair_at(c, axis, far, k, h)],
                    fwd.at[c, k, :, pl.ds(288 * h, 288)], base, axis, sign,
                )
                beside = push(
                    source.at[pair_at(c, axis, (at[axis] + sign + 4) % 4, None, h)],
                    target.at[pair_at(c, axis, at[axis], None, h)],
                    base + 1, axis, sign,
                )
                started[stage, h, c, k] = (halfway, beside)
            own = pair_at(c, axis, at[axis], None, h)
            kept[stage, h, c] = local(
                source.at[own], target.at[own], 1 + (stage * 2 + h) * 2 + c
            )

    def pass_on(stage, h):
        target = (middle, arrived)[stage]
        fwd = (near_fwd, far_fwd)[stage]
        for c in range(2):
            axis = 1 - c if stage == 0 else c
            for k, sign in enumerate((1, -1)):
                base = (((stage * 2 + h) * 2 + c) * 2 + k) * 3
                started[stage, h, c, k][0].wait_recv()
                came = (at[axis] - sign + 4) % 4
                passed[stage, h, c, k] = push(
                    fwd.at[c, k, :, pl.ds(288 * h, 288)],
                    target.at[pair_at(c, axis, came, k, h)], base + 2, axis, sign,
                )

    def finish_stage(stage, h):
        for c in range(2):
            for k in range(2):
                started[stage, h, c, k][1].wait_recv()
                passed[stage, h, c, k].wait_recv()
            kept[stage, h, c].wait()

    for h in range(2):
        send_bundles(0, h)
    for h in range(2):
        pass_on(0, h)
    for h in range(2):
        finish_stage(0, h)
        send_bundles(1, h)
    for h in range(2):
        pass_on(1, h)
    for h in range(2):
        finish_stage(1, h)
    for halfway, beside in started.values():
        halfway.wait_send()
        beside.wait_send()
    for copy in passed.values():
        copy.wait_send()

    row = lax.broadcasted_iota(jnp.int32, (128, 128), 0)
    col = lax.broadcasted_iota(jnp.int32, (128, 128), 1)
    reorder = jnp.where(
        col == ((row >> 2) & 1) * 64 + (row >> 3) * 4 + (row & 3), 1.0, 0.0
    ).astype(BF16)
    second_step = ((lax.broadcasted_iota(jnp.int32, (128, 1), 0) >> 2) & 1) == 1
    position = lax.broadcasted_iota(jnp.int32, (128, 1024), 1)

    def attend(s, carry):
        for j in range(8):
            entry = tab[s, j]
            own = pool[jnp.minimum(entry, 23)]
            came = jnp.maximum(entry - 24, 0)
            moved = arrived[came & 1, came >> 3, (came >> 1) & 3]
            keys[:, j * 128:(j + 1) * 128] = jnp.where(entry < 24, own, moved)
        q = jnp.concatenate([queries[0, s], queries[1, s]], axis=0)
        q = dot(reorder, q)
        q16 = q.astype(BF16)
        scores = dot(q16, keys[...]) * SCALE
        scores = jnp.where(position < lens[s], scores, -jnp.inf)
        new0 = fresh[0, pl.ds(s, 1), :]
        new1 = fresh[1, pl.ds(s, 1), :]
        first = jnp.sum(q * new0, axis=1, keepdims=True) * SCALE
        second = jnp.sum(q * new1, axis=1, keepdims=True) * SCALE
        second = jnp.where(second_step, second, -jnp.inf)
        largest = jnp.maximum(jnp.max(scores, axis=1, keepdims=True), jnp.maximum(first, second))
        weights = jnp.exp(scores - largest)
        first = jnp.exp(first - largest)
        second = jnp.exp(second - largest)
        total = jnp.sum(weights, axis=1, keepdims=True) + first + second
        probs = (weights / total).astype(BF16)
        first = (first / total).astype(BF16).astype(F32)
        second = (second / total).astype(BF16).astype(F32)
        latent = dot_nt(probs, keys[0:LAT, :])
        latent = latent + first * new0[:, 0:LAT] + second * new1[:, 0:LAT]
        lat_send[:, pl.ds(s, 1)] = latent.reshape(16, 1, 8, LAT).astype(BF16)
        return carry

    moves = []
    for half in range(2):
        lax.fori_loop(2 * half, 2 * half + 2, attend, 0)
        pair = pl.ds(2 * half, 2)
        for shift in range(1, groups):
            peer = lax.rem(me + shift, groups)
            slot = half * (groups - 1) + shift - 1
            move = pltpu.make_async_remote_copy(
                src_ref=lat_send.at[peer, pair],
                dst_ref=lat_recv.at[me, pair],
                send_sem=lat_s.at[slot],
                recv_sem=lat_r.at[slot],
                device_id=(peer, lane),
                device_id_type=MESH,
            )
            move.start()
            moves.append(move)
    lat_recv[me] = lat_send[me]
    for move in moves:
        move.wait()

    rows = lat_recv[...].astype(F32).reshape(512, LAT).astype(BF16)
    row = lax.broadcasted_iota(jnp.int32, (128, 512), 0)
    col = lax.broadcasted_iota(jnp.int32, (128, 512), 1)
    base = (row >> 3) * 32 + (row & 3) * 8 + ((row >> 2) & 1) * 4
    heads = []
    for h in range(4):
        up = dot(rows, value_up[h]).astype(BF16)
        take = jnp.where(col == base + h, 1.0, 0.0).astype(BF16)
        heads.append(dot(take, up).astype(BF16))
    heads = jnp.concatenate(heads, axis=1)
    proj_copy.wait()

    def produce(p):
        start, width = PROJ_PARTS[p]
        chunk = 896
        for n in range(width // chunk):
            cols = pl.ds(start + n * chunk, chunk)
            part[:, :, :, cols] = dot(heads, proj[:, cols]).reshape(4, 4, 8, chunk).astype(BF16)

    def finish(p, cols, total):
        wide_sum[:, cols] = total

    ring_sum(
        at, PROJ_ORDERS, ((0, 1), (2, 3)), PROJ_PARTS, part, ((h0l, h0r),),
        ((f0l, f0r),), last, part_s, part_r, neighbour, produce, finish,
    )

    chunk = 1024
    square = jnp.zeros((8, 1), F32)
    for n in range(model // chunk):
        cols = pl.ds(n * chunk, chunk)
        total = wide_sum[:, cols] + jnp.concatenate(
            [resid[0, :, cols].astype(F32), resid[1, :, cols].astype(F32)], axis=0
        )
        stream = total.astype(BF16)
        stream_out[:, cols] = stream
        wide = stream.astype(F32)
        square = square + jnp.sum(wide * wide, axis=1, keepdims=True)
    scale = lax.rsqrt(square * (1.0 / model) + EPS)
    for n in range(model // chunk):
        cols = pl.ds(n * chunk, chunk)
        wide = stream_out[:, cols].astype(F32)
        normed_out[:, cols] = (wide * scale * gain[:, cols]).astype(BF16)


PARTS = ((0, 1280), (2432, 1280), (4864, 1280), (1280, 1152), (3712, 1152), (6144, 1152))
OUT_PARTS = PARTS[:5] + ((6144, 1024),)
STREAMS = ((0, 1, 2), (3, 4, 5))
ROW = 7296


def expert_kernel(
    normed, mix, stream, gate, up, down,
    out,
    rows, hid_w, down_w, acc, obuf,
    h0l, h0r, f0l, f0r, h1l, h1r, f1l, f1r, last,
    g_send, g_recv, s_send, s_recv, w_send, w_recv, w_local,
):
    dp = lax.axis_index("dp")
    tp = lax.axis_index("tp")
    at = (dp // 4, dp % 4, tp // 2)
    core = tp % 2
    signs = (1, -1)
    every = slice(None)

    def neighbour(axis, sign):
        new = list(at)
        new[axis] = (at[axis] + sign + 4) % 4
        return (new[0] * 4 + new[1], new[2] * 2 + core)

    partner = (dp, (tp // 2) * 2 + (1 - core))

    barrier = pltpu.get_barrier_semaphore()
    for axis in range(3):
        for sign in (1, 2, 3):
            pl.semaphore_signal(
                barrier, inc=1, device_id=neighbour(axis, sign), device_id_type=MESH
            )
    pl.semaphore_signal(barrier, inc=1, device_id=partner, device_id_type=MESH)

    rows[at[0], at[1], at[2], :, 0:7168] = normed[...]
    rows[at[0], at[1], at[2], :, 7168:7296] = mix[...]
    local = []
    remote = []

    def spots(e, which):
        if which < 2:
            base = e * 512 + which * 256
            return hid_w.at[:, pl.ds(base, 128)], hid_w.at[:, pl.ds(base + 128, 128)]
        return down_w.at[pl.ds(e * 256, 128)], down_w.at[pl.ds(e * 256 + 128, 128)]

    for e in range(2):
        for which, ref in enumerate((gate, up, down)):
            mine, theirs = spots(e, which)
            n = e * 3 + which
            local.append(pltpu.make_async_copy(ref.at[e], mine, w_local.at[n]))
            remote.append(
                pltpu.make_async_remote_copy(
                    src_ref=ref.at[e],
                    dst_ref=theirs,
                    send_sem=w_send.at[n],
                    recv_sem=w_recv.at[n],
                    device_id=partner,
                    device_id_type=MESH,
                )
            )
    for copy in local:
        copy.start()
    pl.semaphore_wait(barrier, 10)

    order = [(p % 3, (p + 1) % 3, (p + 2) % 3) for p in range(6)]

    def shifted(axis, offset):
        return (at[axis] + offset + 4) % 4

    def block(p, values, start, width):
        where = [None] * 3
        for axis, value in zip(order[p], values):
            where[axis] = every if value is None else value
        return tuple(where) + (every, pl.ds(start, width))

    def known(phase, p, offset):
        values = [None] * phase + [shifted(order[p][phase], offset)]
        return values + [at[axis] for axis in order[p][phase + 1:]]

    def push(phase, p, offset, slot, sign, columns):
        ref = rows.at[block(p, known(phase, p, offset), *columns)]
        slot = (phase * 6 + p) * 4 + slot
        copy = pltpu.make_async_remote_copy(
            src_ref=ref,
            dst_ref=ref,
            send_sem=g_send.at[slot],
            recv_sem=g_recv.at[slot],
            device_id=neighbour(order[p][phase], sign),
            device_id_type=MESH,
        )
        copy.start()
        return copy

    one, two = {}, {}

    def step_one(phase, p):
        if phase == 0:
            for sign in (2, 1, 3):
                two[0, p, sign - 1] = push(0, p, 0, sign - 1, sign, PARTS[p])
            return
        for k in range(3 if phase == 1 else 2):
            two[phase - 1, p, k].wait_recv()
        for k in range(2):
            one[phase, p, k] = push(phase, p, 0, k, signs[k], PARTS[p])

    def step_two(phase, p):
        for k in range(2):
            one[phase, p, k].wait_recv()
            two[phase, p, k] = push(phase, p, -signs[k], 2 + k, signs[k], halves(*PARTS[p])[k])

    for phase in range(3):
        for group in STREAMS:
            for p in group:
                step_one(phase, p)
        if phase == 0:
            for copy in remote:
                copy.start()
            acc[...] = jnp.zeros_like(acc)
        if phase == 1:
            for group in STREAMS:
                for p in group:
                    step_two(phase, p)

    for copy in local:
        copy.wait()
    for copy in remote:
        copy.wait()

    def multiply(p, offset):
        start, width = OUT_PARTS[p]
        lhs = rows[block(p, known(2, p, offset), start, width)]
        lhs = lhs.astype(F32).reshape(128, width).astype(BF16)
        for n in range(4):
            cols = (n * 256, 256)
            where = block(p, known(2, p, offset), *cols)
            product = dot(lhs, hid_w[pl.ds(start, width), pl.ds(*cols)])
            acc[where] = acc[where] + product.reshape(4, 4, 8, 256)

    for p in range(6):
        multiply(p, 0)
    for group in STREAMS:
        for p in group:
            step_two(2, p)
    for p in range(6):
        multiply(p, 1)
        multiply(p, -1)
    for p in range(6):
        for k in range(2):
            two[2, p, k].wait_recv()
        multiply(p, 2)
    for copy in list(one.values()) + list(two.values()):
        copy.wait_send()

    lanes = lax.broadcasted_iota(jnp.int32, (512, 128), 1)
    table = rows[:, :, :, :, 7168:7296].astype(F32).reshape(512, 128)
    hidden = []
    for e in range(2):
        expert = dp * 2 + e
        mine = (lanes == expert) | (lanes == expert + 32)
        weight = jnp.sum(jnp.where(mine, table, 0.0), axis=1, keepdims=True)
        gate_act = acc[:, :, :, :, e * 512:e * 512 + 256].reshape(512, 256)
        up_act = acc[:, :, :, :, e * 512 + 256:e * 512 + 512].reshape(512, 256)
        hidden.append((gate_act / (1.0 + jnp.exp(-gate_act)) * up_act * weight).astype(BF16))
    hidden = jnp.concatenate(hidden, axis=1)

    def produce(p):
        start, width = OUT_PARTS[p]
        for done in range(0, width, 256):
            size = min(256, width - done)
            cols = pl.ds(start + done, size)
            obuf[:, :, :, :, cols] = (
                dot(hidden, down_w[:, cols]).reshape(4, 4, 4, 8, size).astype(BF16)
            )

    def finish(p, cols, total):
        total = total + stream[:, cols].astype(F32)
        out[0, :, cols] = total[0:4].astype(BF16)
        out[1, :, cols] = total[4:8].astype(BF16)

    ring_sum(
        at, [o[::-1] for o in order], STREAMS, OUT_PARTS, obuf, ((h0l, h0r), (h1l, h1r)),
        ((f0l, f0r), (f1l, f1r)), last, s_send, s_recv, neighbour, produce, finish,
    )


def per_device(
    cache_pool, send_plan, tables, lengths, new_latent, queries, value_up, out_proj, residual,
    norm_gain, routes, route_weight, gate_proj, up_proj, down_proj,
):
    model = residual.shape[2]
    vmem = pl.BlockSpec(memory_space=pltpu.VMEM)
    smem = pl.BlockSpec(memory_space=pltpu.SMEM)
    hbm = pl.BlockSpec(memory_space=pl.ANY)
    dma = pltpu.SemaphoreType.DMA


    def rings(parts, shape, width):
        return [pltpu.VMEM((parts,) + shape + (8, width), BF16)] * 2

    scratch = [
        pltpu.VMEM((2, 4, 4, 576, 128), BF16),
        pltpu.VMEM((2, 4, 4, 576, 128), BF16),
        pltpu.VMEM((2, 2, 2, 576, 128), BF16),
        pltpu.VMEM((2, 2, 2, 576, 128), BF16),
        pltpu.VMEM((2, 4, 4, 576, 128), BF16),
        pltpu.VMEM((576, 1024), BF16),
        pltpu.VMEM((2, 4, 576), F32),
        pltpu.VMEM((16, 4, 8, LAT), BF16),
        pltpu.VMEM((16, 4, 8, LAT), BF16),
        pltpu.VMEM((512, model), BF16),
        pltpu.VMEM((4, 4, 8, model), BF16),
        pltpu.VMEM((8, model), F32),
    ]
    scratch += rings(4, (4,), 896)
    scratch += rings(4, (4,), 1792)
    scratch.append(pltpu.VMEM((4, 3, 8, 1792), BF16))
    scratch += [dma((48,)), dma((48,)), dma((30,)), dma((30,)), dma((32,)), dma((32,)), dma((9,))]
    stream, normed, mix = pl.pallas_call(
        attention_kernel,
        out_shape=(
            jax.ShapeDtypeStruct((8, model), BF16),
            jax.ShapeDtypeStruct((8, model), BF16),
            jax.ShapeDtypeStruct((8, 128), BF16),
        ),
        in_specs=[smem, smem, smem, vmem, vmem, vmem, vmem, hbm, vmem, vmem, vmem, vmem],
        out_specs=(vmem, vmem, vmem),
        scratch_shapes=scratch,
        compiler_params=pltpu.CompilerParams(
            collective_id=0, has_side_effects=True, vmem_limit_bytes=56 * MIB
        ),
        name="attention",
    )(
        jnp.transpose(send_plan, (0, 2, 1)), tables, lengths, cache_pool, queries, new_latent, value_up,
        out_proj, residual, norm_gain.reshape(1, model), routes, route_weight,
    )

    scratch = [
        pltpu.VMEM((4, 4, 4, 8, ROW), BF16),
        pltpu.VMEM((model, 1024), BF16),
        pltpu.VMEM((512, model), BF16),
        pltpu.VMEM((4, 4, 4, 8, 1024), F32),
        pltpu.VMEM((4, 4, 4, 8, model), BF16),
    ]
    for shape in ((4, 4), (4,)):
        scratch += rings(6, shape, 640)
        scratch += rings(6, shape, 1280)
    scratch.append(pltpu.VMEM((6, 3, 8, 1280), BF16))
    scratch += [dma((n,)) for n in (72, 72, 72, 72, 6, 6, 6)]
    result = pl.pallas_call(
        expert_kernel,
        out_shape=jax.ShapeDtypeStruct(residual.shape, BF16),
        in_specs=[vmem, vmem, vmem, hbm, hbm, hbm],
        out_specs=vmem,
        scratch_shapes=scratch,
        compiler_params=pltpu.CompilerParams(
            collective_id=1, has_side_effects=True, vmem_limit_bytes=60 * MIB
        ),
        name="experts",
    )(normed, mix, stream, gate_proj, up_proj, down_proj)
    return result


def solution(mesh):
    placed = (
        P(("dp", "tp"), None, None),
        P(("dp", "tp"), None, None),
        P(("dp", "tp"), None),
        P(("dp", "tp")),
        P(None, ("dp", "tp"), None),
        P(None, ("dp", "tp"), None, None),
        P("dp", None, None),
        P("dp", None),
        P(None, ("dp", "tp"), None),
        P(),
        P(None, ("dp", "tp"), None),
        P(None, ("dp", "tp"), None),
        P("dp", None, "tp"),
        P("dp", None, "tp"),
        P("dp", "tp", None),
    )
    return jax.shard_map(
        per_device,
        mesh=mesh,
        in_specs=placed,
        out_specs=P(None, ("dp", "tp"), None),
        check_vma=False,
    )
```

```python
import functools

import jax
import jax.numpy as jnp
from jax import lax
from jax.experimental import pallas as pl
from jax.experimental.pallas import tpu as pltpu
from jax.sharding import PartitionSpec as P

MESH = pl.DeviceIdType.MESH
F32 = jnp.float32
BF16 = jnp.bfloat16
LAT = 512
SCALE = 1.0 / 13.856406460551018
EPS = 1e-06
MIB = 1 << 20


def dot(a, b):
    return jnp.dot(a, b, preferred_element_type=F32)


def dot_nt(a, b):
    return lax.dot_general(a, b, (((1,), (1,)), ((), ())), preferred_element_type=F32)


def halves(start, width):
    tiles = width // 128
    first = (tiles + 1) // 2 * 128
    return (start, first), (start + first, width - first)


def ring_sum(
    at, orders, streams, parts, buf, half_in, full_in, last_in, sends, recvs, neighbour, produce, finish
):
    axes = len(orders[0])
    count = len(parts)
    signs = (1, -1)
    far, near = {}, {}

    def place(phase, p, offset):
        where = [slice(None)] * axes
        for a in orders[p][:phase]:
            where[a] = at[a]
        axis = orders[p][phase]
        where[axis] = (at[axis] + offset + 4) % 4
        return tuple(where) + (slice(None),)

    def landing(refs, phase, p, k, width):
        return refs[phase][k].at[(p,) + (slice(None),) * (axes - phase) + (pl.ds(0, width),)]

    def push(src, dst, slot, axis, sign):
        copy = pltpu.make_async_remote_copy(
            src_ref=src,
            dst_ref=dst,
            send_sem=sends.at[slot],
            recv_sem=recvs.at[slot],
            device_id=neighbour(axis, sign),
            device_id_type=MESH,
        )
        copy.start()
        return copy

    def send_far(phase, p):
        for k in range(2):
            start, width = halves(*parts[p])[k]
            far[phase, p, k] = push(
                buf.at[place(phase, p, 2) + (pl.ds(start, width),)],
                landing(half_in, phase, p, k, width),
                (phase * count + p) * 4 + k, orders[p][phase], signs[k],
            )

    def send_near(phase, p, k):
        far[phase, p, k].wait_recv()
        start, width = halves(*parts[p])[k]
        half = place(phase, p, signs[k]) + (pl.ds(start, width),)
        buf[half] = (
            buf[half].astype(F32) + landing(half_in, phase, p, k, width)[...].astype(F32)
        ).astype(BF16)
        near[phase, p, k] = push(
            buf.at[place(phase, p, signs[k]) + (pl.ds(*parts[p]),)],
            landing(full_in, phase, p, k, parts[p][1]),
            (phase * count + p) * 4 + 2 + k, orders[p][phase], signs[k],
        )

    def send_last(p):
        phase = axes - 1
        for offset in (2, 1, 3):
            far[phase, p, offset] = push(
                buf.at[place(phase, p, offset) + (pl.ds(*parts[p]),)],
                last_in.at[p, offset - 1, :, pl.ds(0, parts[p][1])],
                (phase * count + p) * 4 + offset - 1, orders[p][phase], offset,
            )

    def last_sum(p):
        phase = axes - 1
        total = buf[place(phase, p, 0) + (pl.ds(*parts[p]),)].astype(F32)
        for offset in (1, 3, 2):
            far[phase, p, offset].wait_recv()
            total = total + last_in[p, offset - 1, :, pl.ds(0, parts[p][1])].astype(F32)
        return total

    def own_sum(phase, p):
        where = place(phase, p, 0) + (pl.ds(*parts[p]),)
        total = buf[where].astype(F32)
        for k in range(2):
            near[phase, p, k].wait_recv()
            total = total + landing(full_in, phase, p, k, parts[p][1])[...].astype(F32)
        buf[where] = total.astype(BF16)

    for phase in range(axes - 1):
        for stream in streams:
            for p in stream:
                if phase == 0:
                    produce(p)
                else:
                    own_sum(phase - 1, p)
                send_far(phase, p)
        for stream in streams:
            for p in stream:
                for k in range(2):
                    send_near(phase, p, k)
    for stream in streams:
        for p in stream:
            own_sum(axes - 2, p)
            send_last(p)
    for stream in streams:
        for p in stream:
            finish(p, pl.ds(*parts[p]), last_sum(p))
    for copy in list(far.values()) + list(near.values()):
        copy.wait_send()


PROJ_PARTS = ((0, 1792), (3584, 1792), (1792, 1792), (5376, 1792))
PROJ_ORDERS = ((1, 0), (0, 1), (1, 0), (0, 1))


def attention_kernel(
    plan, tab, lens, pool_hbm, queries_hbm, new_latent, value_up, proj_hbm, resid, gain, routes, route_weight,
    stream_out, normed_out, mix_out,
    pool, queries, outgoing, middle, near_fwd, far_fwd, arrived, keys, fresh, lat_send, lat_recv, proj, part,
    wide_sum, h0l, h0r, f0l, f0r, last,
    mig_s, mig_r, lat_s, lat_r, part_s, part_r, local_sem,
):
    groups = 16
    me = lax.axis_index("dp")
    lane = lax.axis_index("tp")
    at = (me // 4, me % 4)
    model = proj_hbm.shape[1]

    pool_copy = pltpu.make_async_copy(pool_hbm, pool, local_sem.at[9])
    pool_copy.start()

    def neighbour(axis, sign):
        new = list(at)
        new[axis] = (at[axis] + sign + 4) % 4
        return (new[0] * 4 + new[1], lane)

    barrier = pltpu.get_barrier_semaphore()
    for shift in range(1, groups):
        pl.semaphore_signal(
            barrier, inc=1, device_id=(lax.rem(me + shift, groups), lane), device_id_type=MESH
        )

    queries_copy = pltpu.make_async_copy(queries_hbm, queries, local_sem.at[10])
    queries_copy.start()
    proj_copy = pltpu.make_async_copy(proj_hbm, proj, local_sem.at[0])
    proj_copy.start()

    pool_copy.wait()
    for c in range(2):
        def pick(i, carry):
            outgoing[c, i // 4, i % 4] = pool[jnp.maximum(plan[0, c, i], 0)]
            return carry

        lax.fori_loop(0, groups, pick, 0)
    for k in range(2):
        fresh[k] = new_latent[k].astype(F32)

    named = jnp.concatenate([routes[0], routes[1]], axis=0)
    given = jnp.concatenate([route_weight[0], route_weight[1]], axis=0)
    lanes = lax.broadcasted_iota(jnp.int32, (8, 128), 1)
    dense = jnp.zeros((8, 128), F32)
    for k in range(8):
        hit = ((lanes & 31) == named[:, k:k + 1]) & (lanes < 64)
        dense = dense + jnp.where(hit, given[:, k:k + 1], 0.0)
    high = dense.astype(BF16).astype(F32)
    mix_out[...] = jnp.where(lanes < 32, high, dense - high).astype(BF16)
    pl.semaphore_wait(barrier, groups - 1)

    def push(src, dst, slot, axis, sign):
        copy = pltpu.make_async_remote_copy(
            src_ref=src,
            dst_ref=dst,
            send_sem=mig_s.at[slot],
            recv_sem=mig_r.at[slot],
            device_id=neighbour(axis, sign),
            device_id_type=MESH,
        )
        copy.start()
        return copy

    def pair_at(c, axis, value, k, h):
        rest = pl.ds(0, 4) if k is None else pl.ds(2 * k, 2)
        where = (rest, value) if axis == 1 else (value, rest)
        return (c,) + where + (pl.ds(288 * h, 288),)

    def local(src, dst, n):
        copy = pltpu.make_async_copy(src, dst, local_sem.at[n])
        copy.start()
        return copy

    started, passed, kept = {}, {}, {}

    def send_bundles(stage, h):
        source, target = (outgoing, middle) if stage == 0 else (middle, arrived)
        fwd = (near_fwd, far_fwd)[stage]
        for c in range(2):
            axis = 1 - c if stage == 0 else c
            far = (at[axis] + 2) % 4
            for k, sign in enumerate((1, -1)):
                base = (((stage * 2 + h) * 2 + c) * 2 + k) * 3
                halfway = push(
                    source.at[pair_at(c, axis, far, k, h)],
                    fwd.at[c, k, :, pl.ds(288 * h, 288)], base, axis, sign,
                )
                beside = push(
                    source.at[pair_at(c, axis, (at[axis] + sign + 4) % 4, None, h)],
                    target.at[pair_at(c, axis, at[axis], None, h)],
                    base + 1, axis, sign,
                )
                started[stage, h, c, k] = (halfway, beside)
            own = pair_at(c, axis, at[axis], None, h)
            kept[stage, h, c] = local(
                source.at[own], target.at[own], 1 + (stage * 2 + h) * 2 + c
            )

    def pass_on(stage, h):
        target = (middle, arrived)[stage]
        fwd = (near_fwd, far_fwd)[stage]
        for c in range(2):
            axis = 1 - c if stage == 0 else c
            for k, sign in enumerate((1, -1)):
                base = (((stage * 2 + h) * 2 + c) * 2 + k) * 3
                started[stage, h, c, k][0].wait_recv()
                came = (at[axis] - sign + 4) % 4
                passed[stage, h, c, k] = push(
                    fwd.at[c, k, :, pl.ds(288 * h, 288)],
                    target.at[pair_at(c, axis, came, k, h)], base + 2, axis, sign,
                )

    def finish_stage(stage, h):
        for c in range(2):
            for k in range(2):
                started[stage, h, c, k][1].wait_recv()
                passed[stage, h, c, k].wait_recv()
            kept[stage, h, c].wait()

    for h in range(2):
        send_bundles(0, h)
    for h in range(2):
        pass_on(0, h)
    for h in range(2):
        finish_stage(0, h)
        send_bundles(1, h)
    for h in range(2):
        pass_on(1, h)
    for h in range(2):
        finish_stage(1, h)
    for halfway, beside in started.values():
        halfway.wait_send()
        beside.wait_send()
    for copy in passed.values():
        copy.wait_send()

    row = lax.broadcasted_iota(jnp.int32, (128, 128), 0)
    col = lax.broadcasted_iota(jnp.int32, (128, 128), 1)
    reorder = jnp.where(
        col == ((row >> 2) & 1) * 64 + (row >> 3) * 4 + (row & 3), 1.0, 0.0
    ).astype(BF16)
    second_step = ((lax.broadcasted_iota(jnp.int32, (128, 1), 0) >> 2) & 1) == 1
    position = lax.broadcasted_iota(jnp.int32, (128, 1024), 1)

    def attend(s, carry):
        for j in range(8):
            entry = tab[s, j]
            own = pool[jnp.minimum(entry, 23)]
            came = jnp.maximum(entry - 24, 0)
            moved = arrived[came & 1, came >> 3, (came >> 1) & 3]
            keys[:, j * 128:(j + 1) * 128] = jnp.where(entry < 24, own, moved)
        q = jnp.concatenate([queries[0, s], queries[1, s]], axis=0)
        q = dot(reorder, q)
        q16 = q.astype(BF16)
        scores = dot(q16, keys[...]) * SCALE
        scores = jnp.where(position < lens[s], scores, -jnp.inf)
        new0 = fresh[0, pl.ds(s, 1), :]
        new1 = fresh[1, pl.ds(s, 1), :]
        first = jnp.sum(q * new0, axis=1, keepdims=True) * SCALE
        second = jnp.sum(q * new1, axis=1, keepdims=True) * SCALE
        second = jnp.where(second_step, second, -jnp.inf)
        largest = jnp.maximum(jnp.max(scores, axis=1, keepdims=True), jnp.maximum(first, second))
        weights = jnp.exp(scores - largest)
        first = jnp.exp(first - largest)
        second = jnp.exp(second - largest)
        total = jnp.sum(weights, axis=1, keepdims=True) + first + second
        probs = (weights / total).astype(BF16)
        first = (first / total).astype(BF16).astype(F32)
        second = (second / total).astype(BF16).astype(F32)
        latent = dot_nt(probs, keys[0:LAT, :])
        latent = latent + first * new0[:, 0:LAT] + second * new1[:, 0:LAT]
        lat_send[:, pl.ds(s, 1)] = latent.reshape(16, 1, 8, LAT).astype(BF16)
        return carry

    queries_copy.wait()
    moves = []
    for half in range(2):
        lax.fori_loop(2 * half, 2 * half + 2, attend, 0)
        pair = pl.ds(2 * half, 2)
        for shift in range(1, groups):
            peer = lax.rem(me + shift, groups)
            slot = half * (groups - 1) + shift - 1
            move = pltpu.make_async_remote_copy(
                src_ref=lat_send.at[peer, pair],
                dst_ref=lat_recv.at[me, pair],
                send_sem=lat_s.at[slot],
                recv_sem=lat_r.at[slot],
                device_id=(peer, lane),
                device_id_type=MESH,
            )
            move.start()
            moves.append(move)
    lat_recv[me] = lat_send[me]
    for move in moves:
        move.wait()

    rows = lat_recv[...].astype(F32).reshape(512, LAT).astype(BF16)
    row = lax.broadcasted_iota(jnp.int32, (128, 512), 0)
    col = lax.broadcasted_iota(jnp.int32, (128, 512), 1)
    base = (row >> 3) * 32 + (row & 3) * 8 + ((row >> 2) & 1) * 4
    heads = []
    for h in range(4):
        up = dot(rows, value_up[h]).astype(BF16)
        take = jnp.where(col == base + h, 1.0, 0.0).astype(BF16)
        heads.append(dot(take, up).astype(BF16))
    heads = jnp.concatenate(heads, axis=1)
    proj_copy.wait()

    def produce(p):
        start, width = PROJ_PARTS[p]
        chunk = 896
        for n in range(width // chunk):
            cols = pl.ds(start + n * chunk, chunk)
            part[:, :, :, cols] = dot(heads, proj[:, cols]).reshape(4, 4, 8, chunk).astype(BF16)

    def finish(p, cols, total):
        wide_sum[:, cols] = total

    ring_sum(
        at, PROJ_ORDERS, ((0, 1), (2, 3)), PROJ_PARTS, part, ((h0l, h0r),),
        ((f0l, f0r),), last, part_s, part_r, neighbour, produce, finish,
    )

    chunk = 1024
    square = jnp.zeros((8, 1), F32)
    for n in range(model // chunk):
        cols = pl.ds(n * chunk, chunk)
        total = wide_sum[:, cols] + jnp.concatenate(
            [resid[0, :, cols].astype(F32), resid[1, :, cols].astype(F32)], axis=0
        )
        stream = total.astype(BF16)
        stream_out[:, cols] = stream
        wide = stream.astype(F32)
        square = square + jnp.sum(wide * wide, axis=1, keepdims=True)
    scale = lax.rsqrt(square * (1.0 / model) + EPS)
    for n in range(model // chunk):
        cols = pl.ds(n * chunk, chunk)
        wide = stream_out[:, cols].astype(F32)
        normed_out[:, cols] = (wide * scale * gain[:, cols]).astype(BF16)


PARTS = ((0, 1280), (2432, 1280), (4864, 1280), (1280, 1152), (3712, 1152), (6144, 1152))
OUT_PARTS = PARTS[:5] + ((6144, 1024),)
STREAMS = ((0, 1, 2), (3, 4, 5))
ROW = 7296


def expert_kernel(
    normed, mix, stream, gate, up, down,
    out,
    rows, hid_w, down_w, acc, obuf,
    h0l, h0r, f0l, f0r, h1l, h1r, f1l, f1r, last,
    g_send, g_recv, s_send, s_recv, w_send, w_recv, w_local,
):
    dp = lax.axis_index("dp")
    tp = lax.axis_index("tp")
    at = (dp // 4, dp % 4, tp // 2)
    core = tp % 2
    signs = (1, -1)
    every = slice(None)

    def neighbour(axis, sign):
        new = list(at)
        new[axis] = (at[axis] + sign + 4) % 4
        return (new[0] * 4 + new[1], new[2] * 2 + core)

    partner = (dp, (tp // 2) * 2 + (1 - core))

    barrier = pltpu.get_barrier_semaphore()
    for axis in range(3):
        for sign in (1, 2, 3):
            pl.semaphore_signal(
                barrier, inc=1, device_id=neighbour(axis, sign), device_id_type=MESH
            )
    pl.semaphore_signal(barrier, inc=1, device_id=partner, device_id_type=MESH)

    rows[at[0], at[1], at[2], :, 0:7168] = normed[...]
    rows[at[0], at[1], at[2], :, 7168:7296] = mix[...]
    local = []
    remote = []

    def spots(e, which):
        if which < 2:
            base = e * 512 + which * 256
            return hid_w.at[:, pl.ds(base, 128)], hid_w.at[:, pl.ds(base + 128, 128)]
        return down_w.at[pl.ds(e * 256, 128)], down_w.at[pl.ds(e * 256 + 128, 128)]

    for e in range(2):
        for which, ref in enumerate((gate, up, down)):
            mine, theirs = spots(e, which)
            n = e * 3 + which
            local.append(pltpu.make_async_copy(ref.at[e], mine, w_local.at[n]))
            remote.append(
                pltpu.make_async_remote_copy(
                    src_ref=ref.at[e],
                    dst_ref=theirs,
                    send_sem=w_send.at[n],
                    recv_sem=w_recv.at[n],
                    device_id=partner,
                    device_id_type=MESH,
                )
            )
    for copy in local:
        copy.start()
    pl.semaphore_wait(barrier, 10)

    order = [(p % 3, (p + 1) % 3, (p + 2) % 3) for p in range(6)]

    def shifted(axis, offset):
        return (at[axis] + offset + 4) % 4

    def block(p, values, start, width):
        where = [None] * 3
        for axis, value in zip(order[p], values):
            where[axis] = every if value is None else value
        return tuple(where) + (every, pl.ds(start, width))

    def known(phase, p, offset):
        values = [None] * phase + [shifted(order[p][phase], offset)]
        return values + [at[axis] for axis in order[p][phase + 1:]]

    def push(phase, p, offset, slot, sign, columns):
        ref = rows.at[block(p, known(phase, p, offset), *columns)]
        slot = (phase * 6 + p) * 4 + slot
        copy = pltpu.make_async_remote_copy(
            src_ref=ref,
            dst_ref=ref,
            send_sem=g_send.at[slot],
            recv_sem=g_recv.at[slot],
            device_id=neighbour(order[p][phase], sign),
            device_id_type=MESH,
        )
        copy.start()
        return copy

    one, two = {}, {}

    def step_one(phase, p):
        if phase == 0:
            for sign in (2, 1, 3):
                two[0, p, sign - 1] = push(0, p, 0, sign - 1, sign, PARTS[p])
            return
        for k in range(3 if phase == 1 else 2):
            two[phase - 1, p, k].wait_recv()
        for k in range(2):
            one[phase, p, k] = push(phase, p, 0, k, signs[k], PARTS[p])

    def step_two(phase, p):
        for k in range(2):
            one[phase, p, k].wait_recv()
            two[phase, p, k] = push(phase, p, -signs[k], 2 + k, signs[k], halves(*PARTS[p])[k])

    for phase in range(3):
        for group in STREAMS:
            for p in group:
                step_one(phase, p)
        if phase == 0:
            for copy in remote:
                copy.start()
            acc[...] = jnp.zeros_like(acc)
        if phase == 1:
            for group in STREAMS:
                for p in group:
                    step_two(phase, p)

    for copy in local:
        copy.wait()
    for copy in remote:
        copy.wait()

    def multiply(p, offset):
        start, width = OUT_PARTS[p]
        lhs = rows[block(p, known(2, p, offset), start, width)]
        lhs = lhs.astype(F32).reshape(128, width).astype(BF16)
        for n in range(4):
            cols = (n * 256, 256)
            where = block(p, known(2, p, offset), *cols)
            product = dot(lhs, hid_w[pl.ds(start, width), pl.ds(*cols)])
            acc[where] = acc[where] + product.reshape(4, 4, 8, 256)

    for p in range(6):
        multiply(p, 0)
    for group in STREAMS:
        for p in group:
            step_two(2, p)
    for p in range(6):
        multiply(p, 1)
        multiply(p, -1)
    for p in range(6):
        for k in range(2):
            two[2, p, k].wait_recv()
        multiply(p, 2)
    for copy in list(one.values()) + list(two.values()):
        copy.wait_send()

    lanes = lax.broadcasted_iota(jnp.int32, (512, 128), 1)
    table = rows[:, :, :, :, 7168:7296].astype(F32).reshape(512, 128)
    hidden = []
    for e in range(2):
        expert = dp * 2 + e
        mine = (lanes == expert) | (lanes == expert + 32)
        weight = jnp.sum(jnp.where(mine, table, 0.0), axis=1, keepdims=True)
        gate_act = acc[:, :, :, :, e * 512:e * 512 + 256].reshape(512, 256)
        up_act = acc[:, :, :, :, e * 512 + 256:e * 512 + 512].reshape(512, 256)
        hidden.append((gate_act / (1.0 + jnp.exp(-gate_act)) * up_act * weight).astype(BF16))
    hidden = jnp.concatenate(hidden, axis=1)

    def produce(p):
        start, width = OUT_PARTS[p]
        for done in range(0, width, 256):
            size = min(256, width - done)
            cols = pl.ds(start + done, size)
            obuf[:, :, :, :, cols] = (
                dot(hidden, down_w[:, cols]).reshape(4, 4, 4, 8, size).astype(BF16)
            )

    def finish(p, cols, total):
        total = total + stream[:, cols].astype(F32)
        out[0, :, cols] = total[0:4].astype(BF16)
        out[1, :, cols] = total[4:8].astype(BF16)

    ring_sum(
        at, [o[::-1] for o in order], STREAMS, OUT_PARTS, obuf, ((h0l, h0r), (h1l, h1r)),
        ((f0l, f0r), (f1l, f1r)), last, s_send, s_recv, neighbour, produce, finish,
    )


def per_device(
    cache_pool, send_plan, tables, lengths, new_latent, queries, value_up, out_proj, residual,
    norm_gain, routes, route_weight, gate_proj, up_proj, down_proj,
):
    model = residual.shape[2]
    vmem = pl.BlockSpec(memory_space=pltpu.VMEM)
    smem = pl.BlockSpec(memory_space=pltpu.SMEM)
    hbm = pl.BlockSpec(memory_space=pl.ANY)
    dma = pltpu.SemaphoreType.DMA


    def rings(parts, shape, width):
        return [pltpu.VMEM((parts,) + shape + (8, width), BF16)] * 2

    scratch = [
        pltpu.VMEM(cache_pool.shape, BF16),
        pltpu.VMEM(queries.shape, BF16),
        pltpu.VMEM((2, 4, 4, 576, 128), BF16),
        pltpu.VMEM((2, 4, 4, 576, 128), BF16),
        pltpu.VMEM((2, 2, 2, 576, 128), BF16),
        pltpu.VMEM((2, 2, 2, 576, 128), BF16),
        pltpu.VMEM((2, 4, 4, 576, 128), BF16),
        pltpu.VMEM((576, 1024), BF16),
        pltpu.VMEM((2, 4, 576), F32),
        pltpu.VMEM((16, 4, 8, LAT), BF16),
        pltpu.VMEM((16, 4, 8, LAT), BF16),
        pltpu.VMEM((512, model), BF16),
        pltpu.VMEM((4, 4, 8, model), BF16),
        pltpu.VMEM((8, model), F32),
    ]
    scratch += rings(4, (4,), 896)
    scratch += rings(4, (4,), 1792)
    scratch.append(pltpu.VMEM((4, 3, 8, 1792), BF16))
    scratch += [dma((48,)), dma((48,)), dma((30,)), dma((30,)), dma((32,)), dma((32,)), dma((11,))]
    stream, normed, mix = pl.pallas_call(
        attention_kernel,
        out_shape=(
            jax.ShapeDtypeStruct((8, model), BF16),
            jax.ShapeDtypeStruct((8, model), BF16),
            jax.ShapeDtypeStruct((8, 128), BF16),
        ),
        in_specs=[smem, smem, smem, hbm, hbm, vmem, vmem, hbm, vmem, vmem, vmem, vmem],
        out_specs=(vmem, vmem, vmem),
        scratch_shapes=scratch,
        compiler_params=pltpu.CompilerParams(
            collective_id=0, has_side_effects=True, vmem_limit_bytes=56 * MIB
        ),
        name="attention",
    )(
        jnp.transpose(send_plan, (0, 2, 1)), tables, lengths, cache_pool, queries, new_latent, value_up,
        out_proj, residual, norm_gain.reshape(1, model), routes, route_weight,
    )

    scratch = [
        pltpu.VMEM((4, 4, 4, 8, ROW), BF16),
        pltpu.VMEM((model, 1024), BF16),
        pltpu.VMEM((512, model), BF16),
        pltpu.VMEM((4, 4, 4, 8, 1024), F32),
        pltpu.VMEM((4, 4, 4, 8, model), BF16),
    ]
    for shape in ((4, 4), (4,)):
        scratch += rings(6, shape, 640)
        scratch += rings(6, shape, 1280)
    scratch.append(pltpu.VMEM((6, 3, 8, 1280), BF16))
    scratch += [dma((n,)) for n in (72, 72, 72, 72, 6, 6, 6)]
    result = pl.pallas_call(
        expert_kernel,
        out_shape=jax.ShapeDtypeStruct(residual.shape, BF16),
        in_specs=[vmem, vmem, vmem, hbm, hbm, hbm],
        out_specs=vmem,
        scratch_shapes=scratch,
        compiler_params=pltpu.CompilerParams(
            collective_id=1, has_side_effects=True, vmem_limit_bytes=60 * MIB
        ),
        name="experts",
    )(normed, mix, stream, gate_proj, up_proj, down_proj)
    return result


def solution(mesh):
    placed = (
        P(("dp", "tp"), None, None),
        P(("dp", "tp"), None, None),
        P(("dp", "tp"), None),
        P(("dp", "tp")),
        P(None, ("dp", "tp"), None),
        P(None, ("dp", "tp"), None, None),
        P("dp", None, None),
        P("dp", None),
        P(None, ("dp", "tp"), None),
        P(),
        P(None, ("dp", "tp"), None),
        P(None, ("dp", "tp"), None),
        P("dp", None, "tp"),
        P("dp", None, "tp"),
        P("dp", "tp", None),
    )
    return jax.shard_map(
        per_device,
        mesh=mesh,
        in_specs=placed,
        out_specs=P(None, ("dp", "tp"), None),
        check_vma=False,
    )
```
